128 devices in a mesh: row: 8 (over z_lo, x), col: 16 (over y, z_hi, core).
Axes of the slice: x: 4, y: 4, z: 4 (z_hi: 2, z_lo: 2; z = z_hi * 2 + z_lo), core: 2. Of those that a mesh axis runs over, the one named last changes fastest.
Arguments:
- small_weight: bfloat16 [4096, 4096], P(('row', 'col')), may hold values from -0.09375 to 0.09375
- expand_out: bfloat16 [8192, 4096], P(('row', 'col')), may hold values from -0.09375 to 0.09375
- expand_in: bfloat16 [8192, 4096], P('col'), may hold values from -0.09375 to 0.09375
- activations: bfloat16 [4096, 8192], P('row', 'col'), may hold values from -6 to 6
- cotangent: bfloat16 [4096, 8192], P('row', 'col'), may hold values from -0.125 to 0.125
Outputs:
- grown_out: bfloat16 [4096, 8192], P('row', 'col')
- grown_grad: bfloat16 [8192, 8192], P('row', 'col')
The draws below stay inside these ranges and needn't reach their ends.
All inputs are finite; a program needn't handle non-finite values.
Results may differ from the reference program's by a relative error of at most 0.019.
Values may be sent and summed in bfloat16 or wider, within the bound.
A program may use at most 128 MiB of HBM per device.

```python
import jax
import jax.numpy as jnp
from jax import lax

D0 = 4096
D1 = 8192
TOK_ROW = 512
TOKENS = 4096
N_ROW = 8


def strengthened(drawn, own_key, source, target, parts, factor):
    def block_of(position):
        return (jnp.arange(drawn.shape[position]) // (drawn.shape[position] // parts)).reshape((-1,) + (1,) * (drawn.ndim - 1 - position))

    first = jax.random.permutation(own_key, parts)[block_of(target)]
    second = (block_of(target) + parts // 2) % parts
    return jnp.where((block_of(source) == first) | (block_of(source) == second), factor * drawn, drawn)


def block_scale(stream_key, shape, split, low, largest):
    gain, own = 1.0, jax.random.fold_in(stream_key, 6)
    for position, parts in split:
        draws = jnp.exp(jax.random.uniform(jax.random.fold_in(own, position), (parts,), jnp.float32, low / len(split), largest / len(split)))
        gain = gain * jnp.repeat(draws, shape[position] // parts).reshape([-1 if axis == position else 1 for axis in range(len(shape))])
    return gain


def normal_values(stream_key, dims, scale, bound, cuts=(), dtype=jnp.bfloat16):
    values = scale * jax.random.normal(stream_key, dims, jnp.float32)
    if cuts:
        values = values * block_scale(stream_key, dims, cuts, -0.22, 0.18)
    return jnp.clip(values, -bound, bound).astype(dtype)


def gaussian_with(key, dims, scale, bound, shards, heavy, dtype=jnp.bfloat16):
    entries = scale * jax.random.normal(key, dims, jnp.float32)
    if shards:
        entries = entries * block_scale(key, dims, shards, -0.22, 0.18)
    return jnp.clip(strengthened(entries, jax.random.fold_in(key, 3), *heavy), -bound, bound).astype(dtype)


def setup_inputs(seed: int = 0) -> dict:
    arg_keys = jax.random.split(jax.random.key(seed), 6)
    small_weight = normal_values(arg_keys[0], (D0, D0), D0 ** -0.5, 0.09375, ((0, 128),))
    expand_out = normal_values(arg_keys[1], (D1, D0), D0 ** -0.5, 0.09375, ((0, 128),))
    expand_in = normal_values(arg_keys[2], (D1, D0), D0 ** -0.5, 0.09375, ((0, 16),))
    activations = normal_values(arg_keys[3], (TOKENS, D1), 1.0, 6.0, ((0, 8), (1, 16)))
    cotangent = gaussian_with(arg_keys[4], (TOKENS, D1), TOKENS ** -0.5, 0.125, ((0, 8), (1, 16)), (0, 1, 16, 2.0))
    return dict(small_weight=small_weight, expand_out=expand_out, expand_in=expand_in, activations=activations, cotangent=cotangent)


def accumulate(total, pair):
    cot_rows, act_rows = pair
    term = jnp.dot(cot_rows.T, act_rows, preferred_element_type=jnp.float32)
    return total + term.astype(jnp.bfloat16).astype(jnp.float32), None


def reference(small_weight, expand_out, expand_in, activations, cotangent):
    operator = jnp.dot(small_weight, expand_in.T, preferred_element_type=jnp.float32).astype(jnp.bfloat16)
    grown_weight = jnp.dot(expand_out, operator, preferred_element_type=jnp.float32).astype(jnp.bfloat16)
    grown_out = jnp.dot(activations, grown_weight.T, preferred_element_type=jnp.float32).astype(jnp.bfloat16)
    cot_groups = cotangent.reshape(N_ROW, TOK_ROW, D1)
    act_groups = activations.reshape(N_ROW, TOK_ROW, D1)
    total, unused = lax.scan(accumulate, jnp.zeros((D1, D1), jnp.float32), (cot_groups, act_groups))
    return grown_out, total.astype(jnp.bfloat16)
```

```python
import jax
import jax.numpy as jnp
from jax import lax
from jax.experimental import pallas as pl
from jax.experimental.pallas import tpu as pltpu
from jax.sharding import PartitionSpec as P

MESH = pl.DeviceIdType.MESH
F32 = jnp.float32
BF16 = jnp.bfloat16
N_SEM = 96


def dot(a, b, dims):
    return lax.dot_general(a, b, (dims, ((), ())), preferred_element_type=F32)


def kernel(
    sw, eo, ei, act, cot, out_ref, grad_ref,
    s_all, e_all, a_all, c_all, c1_in,
    t_sib, t_sib_in, t_own, t_part, t_tmp, t_two, t_swap, t_swap_in, t_all,
    u_own, u_sib, u_sib_in, u_part, u_in, u_all,
    o_part, o_tmp, o_two, g_part, g_tmp, g_two,
    ssem, rsem,
):
    row, col = lax.axis_index("row"), lax.axis_index("col")
    x, zl = row % 4, row // 4
    k, zh, y = col % 2, (col // 2) % 2, col // 4
    z = zh * 2 + zl
    y0, y1, x0, x1 = y % 2, y // 2, x % 2, x // 2

    def at(x=x, y=y, z=z, k=k):
        return ((z % 2) * 4 + x, (y * 2 + z // 2) * 2 + k)

    def ring(i, d):
        return (i + d) % 4

    def outer(i):
        return ring(i, 3 + 2 * (i % 2))

    sib = at(k=1 - k)
    x_up, x_down = at(x=ring(x, 1)), at(x=ring(x, 3))
    y_up, y_down = at(y=ring(y, 1)), at(y=ring(y, 3))
    z_up, z_down = at(z=ring(z, 1)), at(z=ring(z, 3))
    z_far = at(z=ring(z, 2))

    own_step = 1 - 2 * zh
    c_to = [
        at(x=2 * y0 + zh),
        at(x=2 * y0 + zh, y=ring(y, 4 + own_step)),
        at(x=2 * y0 + 1 - zh),
        at(x=2 * y0 + 1 - zh, y=ring(y, 4 - own_step)),
    ]
    c_slot = [y, ring(y, 4 + own_step), y, ring(y, 4 - own_step)]
    c_self = [x == 2 * y0 + zh, None, x == 2 * y0 + 1 - zh, None]
    c_home = x1 == y0
    c_src_y = jnp.where(c_home, y, ring(y, 4 - (1 - 2 * x0)))
    e_x = jnp.where(zh == 0, x, outer(x))
    e_y = zl * 2 + x1
    e_home = x1 == y0
    e_src_x = jnp.where(e_home, x, outer(x))
    e_src_z = jnp.where(e_home, 0, 2) + y1

    barrier = pltpu.get_barrier_semaphore()

    def greet(to):
        pl.semaphore_signal(barrier, inc=1, device_id=to, device_id_type=MESH)

    expected = 0
    for dz in range(4):
        for dk in range(2):
            if dz or dk:
                greet(at(z=ring(z, dz), k=(k + dk) % 2))
                expected += 1
    for to in (x_up, x_down, y_up, y_down):
        greet(to)
        expected += 1

    def greet_unless_self(to):
        other = jnp.logical_or(to[0] != row, to[1] != col)

        @pl.when(other)
        def _():
            greet(to)

        return other.astype(jnp.int32)

    for to in c_to:
        expected += greet_unless_self(to)
    for i in range(4):
        expected += greet_unless_self(at(x=i, y=c_src_y))
    for i in range(4):
        expected += greet_unless_self(at(x=e_x, y=e_y, z=i, k=y1))
    for i in range(4):
        expected += greet_unless_self(at(x=e_src_x, y=2 * k + i // 2, z=e_src_z, k=i % 2))
    pl.semaphore_wait(barrier, expected)

    count = [0]
    sent = []

    def ids(n):
        first = count[0]
        count[0] += n
        assert count[0] <= N_SEM
        return first

    def remote(src, dst, to, s, r=None):
        return pltpu.make_async_remote_copy(
            src_ref=src, dst_ref=dst, send_sem=ssem.at[s], recv_sem=rsem.at[s if r is None else r],
            device_id=to, device_id_type=MESH,
        )

    def send(src, dst, to, s, r=None):
        copy = remote(src, dst, to, s, r)
        copy.start()
        sent.append((copy, None))

    def send_or_copy(src, dst, to, s, r):
        mine = jnp.logical_and(to[0] == row, to[1] == col)
        copy = remote(src, dst, to, s, r)

        @pl.when(mine)
        def _():
            pltpu.make_async_copy(src, dst, rsem.at[r]).start()

        @pl.when(jnp.logical_not(mine))
        def _():
            copy.start()

        sent.append((copy, jnp.logical_not(mine)))

    def arrived(ref, r):
        remote(ref, ref, sib, r).wait_recv()

    class Gather:
        def __init__(self, slot, first, second, me, up, down):
            self.slot, self.first, self.second, self.me = slot, first, second, me
            self.up, self.down, self.s = up, down, ids(4)

        def start(self):
            mine = self.slot(self.me)
            send(mine, mine, self.up, self.s)
            send(mine, mine, self.down, self.s + 1)

        def pass_up(self):
            i = ring(self.me, 3)
            arrived(self.slot(i), self.s)
            send(self.first(i), self.first(i), self.up, self.s + 2)

        def pass_down(self):
            i = ring(self.me, 1)
            arrived(self.slot(i), self.s + 1)
            send(self.second(i), self.second(i), self.down, self.s + 3)

        def finish(self):
            i = ring(self.me, 2)
            arrived(self.first(i), self.s + 2)
            arrived(self.second(i), self.s + 3)

    class Scatter:
        def __init__(self, slot, first, second, tmp, two, me, up, down):
            self.slot, self.first, self.second = slot, first, second
            self.tmp, self.two, self.me, self.up, self.down, self.s = tmp, two, me, up, down, ids(4)

        def start(self):
            i = ring(self.me, 2)
            send(self.first(i), self.tmp.at[0], self.up, self.s)
            send(self.second(i), self.tmp.at[1], self.down, self.s + 1)

        def pass_up(self):
            i = ring(self.me, 1)
            arrived(self.tmp.at[0], self.s)
            add_into(self.first(i), self.tmp.at[0])
            send(self.slot(i), self.two.at[0], self.up, self.s + 2)

        def pass_down(self):
            i = ring(self.me, 3)
            arrived(self.tmp.at[1], self.s + 1)
            add_into(self.second(i), self.tmp.at[1])
            send(self.slot(i), self.two.at[1], self.down, self.s + 3)

        def finish(self):
            arrived(self.two.at[0], self.s + 2)
            arrived(self.two.at[1], self.s + 3)

    def add_into(dst, src):
        rows = dst.shape[0]

        @pl.loop(0, rows // 64)
        def _(i):
            part = pl.ds(pl.multiple_of(i * 64, 64), 64)
            dst[part] = (dst[part].astype(F32) + src[part].astype(F32)).astype(BF16)

    c1 = ids(1)
    send(cot.at[1 - zh], c1_in, z_far, c1)
    c2s, c2r = ids(4), ids(4)
    for half in range(2):
        send_or_copy(cot.at[zh, half], c_all.at[k, c_slot[half], x], c_to[half], c2s + half, c2r + x)
    a1 = ids(1)
    send(act.at[1 - zh], a_all.at[:, x, :, pl.ds(pl.multiple_of(zh * 512, 512), 512)], z_far, a1)
    s1 = ids(8)
    s_home = s_all.at[zl, x, pl.ds(pl.multiple_of(zh * 64 + k * 32, 32), 32)]
    for dz in (1, 3, 2, 0):
        for dk in range(2):
            tz, tk = ring(z, dz), (k + dk) % 2
            piece = sw.at[:, pl.ds(pl.multiple_of(((tz // 2) * 2 + tk) * 1024, 1024), 1024)]
            if dz or dk:
                send(piece, s_home, at(z=tz, k=tk), s1 + dz * 2 + dk)
            else:
                pltpu.make_async_copy(piece, s_home, rsem.at[s1]).start()
    e1s, e1r = ids(4), ids(4)
    for i in range(4):
        send_or_copy(
            eo.at[:, i * 1024:(i + 1) * 1024], e_all.at[e_x, y0 * 2 + k],
            at(x=e_x, y=e_y, z=i, k=y1), e1s + i, e1r + y0 * 2 + k,
        )
    a_own = ids(1)
    own_cols = a_all.at[:, x, :, pl.ds(pl.multiple_of(zh * 512, 512), 512)]
    pltpu.make_async_copy(act.at[zh], own_cols, rsem.at[a_own]).start()

    acts = act[...].reshape(512, 512)

    def t_block(yy, half, kk):
        cols = pl.ds(pl.multiple_of((half * 2 + kk) * 1024 + yy * 256, 256), 256)
        return dot(acts, ei[:, cols], ((1,), (0,)))

    order = (2, 1, 3, 0)
    t1 = ids(4)
    for d in order:
        for half in range(2):
            t_sib[d, half] = t_block(ring(y, d), half, 1 - k).astype(BF16)
        send(t_sib.at[d], t_sib_in.at[d], sib, t1 + d)
    for d in order:
        for half in range(2):
            t_own[d, half] = t_block(ring(y, d), half, k)

    def t_join(d):
        arrived(t_sib_in.at[d], t1 + d)
        for half in range(2):
            t_part[ring(y, d), half] = (t_own[d, half] + t_sib_in[d, half].astype(F32)).astype(BF16)

    t_sum = Scatter(
        lambda i: t_part.at[i], lambda i: t_part.at[i, 0], lambda i: t_part.at[i, 1], t_tmp, t_two, y, y_up, y_down
    )
    t_join(2)
    t_sum.start()

    arrived(c1_in, c1)
    for half in range(2):
        send_or_copy(
            c1_in.at[half], c_all.at[k, c_slot[2 + half], x], c_to[2 + half], c2s + 2 + half, c2r + x
        )
    t_join(1)
    t_join(3)
    t_sum.pass_up()
    t_sum.pass_down()
    t_join(0)

    for i in range(8):
        arrived(s_home, s1 + i)
    s_ring = Gather(lambda i: s_all.at[:, i], lambda i: s_all.at[0, i], lambda i: s_all.at[1, i], x, x_up, x_down)
    s_ring.start()
    for i in range(4):
        arrived(c_all.at[k, y, i], c2r + i)
    c_ring = Gather(
        lambda i: c_all.at[k, i], lambda i: c_all.at[k, i, 0:2], lambda i: c_all.at[k, i, 2:4], y, y_up, y_down
    )
    c_ring.start()
    c4 = ids(5)
    send(c_all.at[k, y], c_all.at[k, y], sib, c4)
    arrived(own_cols, a_own)
    arrived(a_all.at[:, x, :, pl.ds(pl.multiple_of((1 - zh) * 512, 512), 512)], a1)
    a_ring = Gather(lambda i: a_all.at[:, i], lambda i: a_all.at[0, i], lambda i: a_all.at[1, i], x, x_up, x_down)
    a_ring.start()
    for i in range(4):
        arrived(e_all.at[x, i], e1r + i)
    e_ring = Gather(
        lambda i: e_all.at[i], lambda i: e_all.at[i, 0:2], lambda i: e_all.at[i, 2:4], x, x_up, x_down
    )
    e_ring.start()

    t_sum.finish()
    for half in range(2):
        t_own[0, half] = t_part[y, half].astype(F32) + t_two[0, half].astype(F32) + t_two[1, half].astype(F32)
    t_swap[...] = t_own[0, 1 - zh].astype(BF16)
    t3 = ids(1)
    send(t_swap, t_swap_in, z_far, t3)
    s_ring.pass_up()
    s_ring.pass_down()
    arrived(t_swap_in, t3)
    t_all[y] = (t_own[0, zh] + t_swap_in[...].astype(F32)).astype(BF16)
    t_ring = Gather(
        lambda i: t_all.at[i], lambda i: t_all.at[i, 0:256], lambda i: t_all.at[i, 256:512], y, y_up, y_down
    )
    t_ring.start()
    c_ring.pass_up()
    c_ring.pass_down()
    for n, d in ((1, 3), (2, 1)):
        send(c_all.at[k, ring(y, d)], c_all.at[k, ring(y, d)], sib, c4 + n)
    t_ring.pass_up()
    t_ring.pass_down()
    a_ring.pass_up()
    a_ring.pass_down()
    s_ring.finish()
    t_ring.finish()

    def u_block(n):
        total = None
        for i in range(4):
            part = dot(t_all[i], s_all[n // 4, n % 4, :, i * 256:(i + 1) * 256], ((1,), (1,)))
            total = part if total is None else total + part
        return total

    u1 = ids(1)
    for n in range(8):
        u_own[n % 2, n // 2] = u_block(n)
    u_sib[...] = u_own[1 - k].astype(BF16)
    send(u_sib, u_sib_in, sib, u1)
    e_ring.pass_up()
    e_ring.pass_down()
    arrived(u_sib_in, u1)
    u_part[...] = (u_own[k] + u_sib_in[...].astype(F32)).astype(BF16)
    u2 = ids(4)
    for d in (1, 3, 2):
        send(u_part.at[ring(z, d)], u_in.at[d], at(z=ring(z, d)), u2 + d)
    c_ring.finish()
    for n, half in ((3, slice(0, 2)), (4, slice(2, 4))):
        send(c_all.at[k, ring(y, 2), half], c_all.at[k, ring(y, 2), half], sib, c4 + n)
    for d in (1, 3, 2):
        arrived(u_in.at[d], u2 + d)

    def u_cols(kk, i):
        return pl.ds(pl.multiple_of(kk * 512 + i * 128, 128), 128)

    u_all[zl, :, u_cols(k, y)] = (u_part[z].astype(F32) + u_in[2].astype(F32)).astype(BF16)
    u_all[1 - zl, :, u_cols(k, y)] = (u_in[1].astype(F32) + u_in[3].astype(F32)).astype(BF16)
    u_ring = Gather(
        lambda i: u_all.at[:, :, u_cols(k, i)],
        lambda i: u_all.at[0, :, u_cols(k, i)],
        lambda i: u_all.at[1, :, u_cols(k, i)],
        y, y_up, y_down,
    )
    u_ring.start()
    u4 = ids(5)
    send(u_ring.slot(y), u_ring.slot(y), sib, u4)

    a_ring.finish()
    for n, d in ((0, 0), (1, 3), (2, 1)):
        arrived(c_all.at[1 - k, ring(y, d)], c4 + n)
    for n, half in ((3, slice(0, 2)), (4, slice(2, 4))):
        arrived(c_all.at[1 - k, ring(y, 2), half], c4 + n)

    @pl.loop(0, 8)
    def _(n):
        v, kk, half = n // 4, (n // 2) % 2, n % 2
        home = 2 * v + x1
        away = ring(home, 4 + 1 - 2 * x0)
        cols = pl.ds(pl.multiple_of(half * 512, 512), 512)
        total = dot(
            c_all[kk, home].reshape(512, 512), a_all[0, :, :, cols].reshape(512, 512), ((0,), (0,))
        ) + dot(c_all[kk, away].reshape(512, 512), a_all[1, :, :, cols].reshape(512, 512), ((0,), (0,)))
        g_part[half * 2 + v, pl.ds(pl.multiple_of(kk * 512, 512), 512)] = total.astype(BF16)

    g_sum = Scatter(
        lambda i: g_part.at[i], lambda i: g_part.at[i, 0:512], lambda i: g_part.at[i, 512:1024],
        g_tmp, g_two, z, z_up, z_down,
    )
    g_sum.start()

    u_ring.pass_up()
    u_ring.pass_down()
    for n, d in ((1, 3), (2, 1)):
        send(u_ring.slot(ring(y, d)), u_ring.slot(ring(y, d)), sib, u4 + n)
    e_ring.finish()
    g_sum.pass_up()
    g_sum.pass_down()
    u_ring.finish()
    for n in range(2):
        half = u_all.at[n, :, u_cols(k, ring(y, 2))]
        send(half, half, sib, u4 + 3 + n)
    for n, d in ((0, 0), (1, 3), (2, 1)):
        arrived(u_all.at[:, :, u_cols(1 - k, ring(y, d))], u4 + n)
    for n in range(2):
        arrived(u_all.at[n, :, u_cols(1 - k, ring(y, 2))], u4 + 3 + n)
    for v in range(2):
        for w in range(2):
            slot = 2 * y0 + v
            if w:
                slot = outer(slot)
            weight = e_all[slot].reshape(256, 1024)
            for tok in range(2):
                total = dot(u_all[tok], weight, ((1,), (1,))).astype(BF16)
                for n in range(2):
                    o_part[v * 2 + tok, :, n * 256 + w * 128:n * 256 + w * 128 + 128] = total[:, n * 128:n * 128 + 128]
    o_sum = Scatter(
        lambda i: o_part.at[i], lambda i: o_part.at[i, 0:256], lambda i: o_part.at[i, 256:512],
        o_tmp, o_two, z, z_up, z_down,
    )
    o_sum.start()
    o_sum.pass_up()
    o_sum.pass_down()

    def last(dst, part, two):
        @pl.loop(0, dst.shape[0] // 64)
        def _(i):
            rows = pl.ds(pl.multiple_of(i * 64, 64), 64)
            dst[rows] = (
                part[rows].astype(F32) + two[0, rows].astype(F32) + two[1, rows].astype(F32)
            ).astype(BF16)

    g_sum.finish()
    last(grad_ref, g_part.at[z], g_two)
    o_sum.finish()
    last(out_ref, o_part.at[z], o_two)
    for copy, when in sent:
        if when is None:
            copy.wait_send()
        else:
            pl.when(when)(copy.wait_send)


def per_device(small_weight, expand_out, expand_in, activations, cotangent):
    vmem = pl.BlockSpec(memory_space=pltpu.VMEM)

    def buf(*shape, dtype=BF16):
        return pltpu.VMEM(shape, dtype)

    return pl.pallas_call(
        kernel,
        out_shape=(
            jax.ShapeDtypeStruct((512, 512), BF16),
            jax.ShapeDtypeStruct((1024, 512), BF16),
        ),
        in_specs=[vmem] * 5,
        out_specs=(vmem, vmem),
        scratch_shapes=[
            buf(2, 4, 128, 1024),
            buf(4, 4, 64, 1024),
            buf(2, 4, 128, 1024),
            buf(2, 4, 4, 128, 512),
            buf(2, 128, 512),
            buf(4, 2, 512, 256),
            buf(4, 2, 512, 256),
            buf(4, 2, 512, 256, dtype=F32),
            buf(4, 2, 512, 256),
            buf(2, 512, 256),
            buf(2, 2, 512, 256),
            buf(512, 256),
            buf(512, 256),
            buf(4, 512, 256),
            buf(2, 4, 512, 128, dtype=F32),
            buf(4, 512, 128),
            buf(4, 512, 128),
            buf(4, 512, 128),
            buf(4, 512, 128),
            buf(2, 512, 1024),
            buf(4, 512, 512),
            buf(2, 256, 512),
            buf(2, 512, 512),
            buf(4, 1024, 512),
            buf(2, 512, 512),
            buf(2, 1024, 512),
            pltpu.SemaphoreType.DMA((N_SEM,)),
            pltpu.SemaphoreType.DMA((N_SEM,)),
        ],
        compiler_params=pltpu.CompilerParams(
            collective_id=0, has_side_effects=True, vmem_limit_bytes=58 * 2**20
        ),
        cost_estimate=pl.CostEstimate(flops=9_700_000_000, bytes_accessed=8_000_000, transcendentals=0),
        name="grow",
    )(
        small_weight,
        expand_out,
        expand_in,
        activations.reshape(2, 2, 128, 512),
        cotangent.reshape(2, 2, 128, 512),
    )


def solution(mesh):
    in_specs = (
        P(("row", "col"), None),
        P(("row", "col"), None),
        P("col", None),
        P("row", "col"),
        P("row", "col"),
    )
    out_specs = (P("row", "col"), P("row", "col"))
    return jax.shard_map(per_device, mesh=mesh, in_specs=in_specs, out_specs=out_specs, check_vma=False)
```

```python
import jax
import jax.numpy as jnp
from jax import lax
from jax.experimental import pallas as pl
from jax.experimental.pallas import tpu as pltpu
from jax.sharding import PartitionSpec as P

MESH = pl.DeviceIdType.MESH
F32 = jnp.float32
BF16 = jnp.bfloat16
N_SEM = 160


def dot(a, b, dims):
    return lax.dot_general(a, b, (dims, ((), ())), preferred_element_type=F32)


def kernel(
    sw, eo, ei_hbm, act_hbm, cot, out_ref, grad_ref,
    ei, act, in_sem, s_all, e_z, e_all, out_v, grad_v, out_sem, a_all, c_all, c_spread, c1_in,
    t_sib, t_sib_in, t_own, t_part, t_tmp, t_two, t_swap, t_swap_in, t_all,
    u_own, u_sib, u_sib_in, u_part, u_in, u_all,
    o_part, o_tmp, o_two, g_part, g_tmp, g_two,
    ssem, rsem,
):
    row, col = lax.axis_index("row"), lax.axis_index("col")
    x, zl = row % 4, row // 4
    k, zh, y = col % 2, (col // 2) % 2, col // 4
    z = zh * 2 + zl
    y0, y1, x0, x1 = y % 2, y // 2, x % 2, x // 2

    def at(x=x, y=y, z=z, k=k):
        return ((z % 2) * 4 + x, (y * 2 + z // 2) * 2 + k)

    def ring(i, d):
        return (i + d) % 4

    def outer(i):
        return ring(i, 3 + 2 * (i % 2))

    sib = at(k=1 - k)
    x_up, x_down = at(x=ring(x, 1)), at(x=ring(x, 3))
    y_up, y_down = at(y=ring(y, 1)), at(y=ring(y, 3))
    z_up, z_down = at(z=ring(z, 1)), at(z=ring(z, 3))
    z_far = at(z=ring(z, 2))

    c_x = [[2 * y0 + zh, 2 * (1 - y0) + zh], [2 * y0 + 1 - zh, 2 * (1 - y0) + 1 - zh]]
    c_home = x1 == y0
    e_x = [x, x, outer(x), outer(x)]
    e_to = [at(x=e_x[i], y=(i % 2) * 2 + x1, k=y1) for i in range(4)]
    e_src_x = jnp.where(c_home, x, outer(x))

    order = (2, 1, 3, 0)
    act_copy = pltpu.make_async_copy(act_hbm, act, in_sem.at[16])
    act_copy.start()

    def ei_copies(d):
        return [
            pltpu.make_async_copy(
                ei_hbm.at[:, pl.ds(pl.multiple_of(q * 1024 + ring(y, d) * 256, 256), 256)], ei.at[d, q], in_sem.at[d * 4 + q]
            )
            for q in range(4)
        ]

    def a_cols(half):
        return pl.ds(pl.multiple_of(half * 512, 512), 512)

    a_own_copy = pltpu.make_async_copy(act_hbm.at[zh], a_all.at[:, x, :, a_cols(zh)], in_sem.at[17])
    a_own_copy.start()
    for d in order:
        for copy in ei_copies(d):
            copy.start()

    barrier = pltpu.get_barrier_semaphore()

    def greet(to):
        pl.semaphore_signal(barrier, inc=1, device_id=to, device_id_type=MESH)

    expected = 0
    for dz in range(4):
        for dk in range(2):
            if dz or dk:
                greet(at(z=ring(z, dz), k=(k + dk) % 2))
                expected += 1
    for to in (x_up, x_down, y_up, y_down):
        greet(to)
        expected += 1

    def greet_unless_self(to):
        other = jnp.logical_or(to[0] != row, to[1] != col)

        @pl.when(other)
        def _():
            greet(to)

        return other.astype(jnp.int32)

    for d in (2,):
        greet(at(x=ring(x, d)))
        expected += 1
    for to in e_to:
        expected += greet_unless_self(to)
    for i in range(4):
        expected += greet_unless_self(at(x=e_src_x, y=2 * k + i // 2, k=i % 2))
    count = [0]
    sent = []

    def ids(n):
        first = count[0]
        count[0] += n
        assert count[0] <= N_SEM
        return first

    def remote(src, dst, to, s, r=None):
        return pltpu.make_async_remote_copy(
            src_ref=src, dst_ref=dst, send_sem=ssem.at[s], recv_sem=rsem.at[s if r is None else r],
            device_id=to, device_id_type=MESH,
        )

    def send(src, dst, to, s, r=None):
        copy = remote(src, dst, to, s, r)
        copy.start()
        sent.append((copy, None))

    def send_or_copy(src, dst, to, s, r):
        mine = jnp.logical_and(to[0] == row, to[1] == col)
        copy = remote(src, dst, to, s, r)

        @pl.when(mine)
        def _():
            pltpu.make_async_copy(src, dst, rsem.at[r]).start()

        @pl.when(jnp.logical_not(mine))
        def _():
            copy.start()

        sent.append((copy, jnp.logical_not(mine)))

    def arrived(ref, r):
        remote(ref, ref, sib, r).wait_recv()

    class Gather:
        def __init__(self, slot, first, second, me, up, down):
            self.slot, self.first, self.second, self.me = slot, first, second, me
            self.up, self.down, self.s = up, down, ids(4)

        def start(self):
            mine = self.slot(self.me)
            send(mine, mine, self.up, self.s)
            send(mine, mine, self.down, self.s + 1)

        def pass_up(self):
            i = ring(self.me, 3)
            arrived(self.slot(i), self.s)
            send(self.first(i), self.first(i), self.up, self.s + 2)

        def pass_down(self):
            i = ring(self.me, 1)
            arrived(self.slot(i), self.s + 1)
            send(self.second(i), self.second(i), self.down, self.s + 3)

        def finish(self):
            i = ring(self.me, 2)
            arrived(self.first(i), self.s + 2)
            arrived(self.second(i), self.s + 3)

    class Scatter:
        def __init__(self, slot, first, second, tmp, two, me, up, down):
            self.slot, self.first, self.second = slot, first, second
            self.tmp, self.two, self.me, self.up, self.down, self.s = tmp, two, me, up, down, ids(4)

        def start(self):
            i = ring(self.me, 2)
            send(self.first(i), self.tmp.at[0], self.up, self.s)
            send(self.second(i), self.tmp.at[1], self.down, self.s + 1)

        def pass_up(self):
            i = ring(self.me, 1)
            arrived(self.tmp.at[0], self.s)
            add_into(self.first(i), self.tmp.at[0])
            send(self.slot(i), self.two.at[0], self.up, self.s + 2)

        def pass_down(self):
            i = ring(self.me, 3)
            arrived(self.tmp.at[1], self.s + 1)
            add_into(self.second(i), self.tmp.at[1])
            send(self.slot(i), self.two.at[1], self.down, self.s + 3)

        def finish(self):
            arrived(self.two.at[0], self.s + 2)
            arrived(self.two.at[1], self.s + 3)

    def add_into(dst, src):
        rows = dst.shape[0]

        @pl.loop(0, rows // 64)
        def _(i):
            part = pl.ds(pl.multiple_of(i * 64, 64), 64)
            dst[part] = (dst[part].astype(F32) + src[part].astype(F32)).astype(BF16)

    sp, c1, a1, s1, e1, e2s, e2r = ids(2), ids(2), ids(1), ids(8), ids(4), ids(4), ids(4)
    c2s, c2r = [ids(4), ids(4)], [ids(4), ids(4)]
    t1, t3, u1 = ids(4), ids(2), ids(2)
    u2, u4 = [ids(4), ids(4)], [ids(5), ids(5)]
    c4 = [ids(5), ids(5)]
    s_home = s_all.at[zl, x, pl.ds(pl.multiple_of(zh * 64 + k * 32, 32), 32)]

    def spread_send():
        for n, to in enumerate((y_up, y_down)):
            send(cot.at[:, 1, n * 64:n * 64 + 64], c_spread.at[:, n * 64:n * 64 + 64], to, sp + n)

    def c1_send(half):
        src = cot.at[1 - zh, 0] if half == 0 else c_spread.at[1 - zh]
        send(src, c1_in.at[half], z_far, c1 + half)

    def a1_send():
        send(act_hbm.at[1 - zh], a_all.at[:, x, :, a_cols(zh)], z_far, a1)

    def c2_send(other, half):
        if other:
            src = c1_in.at[half]
        else:
            src = c_spread.at[zh] if half else cot.at[zh, 0]
        for j in range(2):
            send_or_copy(
                src.at[:, j * 256:(j + 1) * 256], c_all.at[k, j, y, x], at(x=c_x[other][half]),
                c2s[j] + 2 * other + half, c2r[j] + x,
            )

    def s1_send():
        for dz in (1, 3, 2, 0):
            for dk in range(2):
                tz, tk = ring(z, dz), (k + dk) % 2
                piece = sw.at[:, pl.ds(pl.multiple_of(((tz // 2) * 2 + tk) * 1024, 1024), 1024)]
                if dz or dk:
                    send(piece, s_home, at(z=tz, k=tk), s1 + dz * 2 + dk)
                else:
                    pltpu.make_async_copy(piece, s_home, rsem.at[s1]).start()

    def e1_send():
        for d in (1, 3, 2, 0):
            i = ring(z, d)
            piece = eo.at[:, pl.ds(pl.multiple_of(i * 1024, 1024), 1024)]
            if d:
                send(piece, e_z.at[z], at(z=i), e1 + d)
            else:
                pltpu.make_async_copy(piece, e_z.at[z], rsem.at[e1]).start()

    def e2_send():
        for d in range(4):
            arrived(e_z.at[ring(z, 4 - d)], e1 + d)
        for i in range(4):
            send_or_copy(e_z.at[i], e_all.at[e_x[i], y0 * 2 + k], e_to[i], e2s + i, e2r + y0 * 2 + k)

    def e_enter():
        for i in range(4):
            arrived(e_all.at[x, i], e2r + i)
        e_ring.start()

    s_ring = Gather(lambda i: s_all.at[:, i], lambda i: s_all.at[0, i], lambda i: s_all.at[1, i], x, x_up, x_down)
    a_ring = [
        Gather(
            lambda i, c=c: a_all.at[:, i, :, c], lambda i, c=c: a_all.at[0, i, :, c],
            lambda i, c=c: a_all.at[1, i, :, c], x, x_up, x_down,
        )
        for c in (a_cols(zh), a_cols(1 - zh))
    ]
    e_ring = Gather(
        lambda i: e_all.at[i], lambda i: e_all.at[i, 0:2], lambda i: e_all.at[i, 2:4], x, x_up, x_down
    )
    c_ring = [
        Gather(
            lambda i, j=j: c_all.at[k, j, i], lambda i, j=j: c_all.at[k, j, i, 0:2],
            lambda i, j=j: c_all.at[k, j, i, 2:4], y, y_up, y_down,
        )
        for j in range(2)
    ]
    t_ring = [
        Gather(
            lambda i, c=c: t_all.at[i, c * 256:c * 256 + 256], lambda i, c=c: t_all.at[i, c * 256:c * 256 + 128],
            lambda i, c=c: t_all.at[i, c * 256 + 128:c * 256 + 256], y, y_up, y_down,
        )
        for c in range(2)
    ]

    def u_cols(kk, i):
        return pl.ds(pl.multiple_of(kk * 512 + i * 128, 128), 128)

    def u_block(c, kk, i, tok=slice(None)):
        return u_all.at[tok, c * 256:c * 256 + 256, u_cols(kk, i)]

    u_ring = [
        Gather(
            lambda i, c=c: u_block(c, k, i), lambda i, c=c: u_block(c, k, i, 0), lambda i, c=c: u_block(c, k, i, 1),
            y, y_up, y_down,
        )
        for c in range(2)
    ]
    t_sum = Scatter(
        lambda i: t_part.at[i], lambda i: t_part.at[i, 0], lambda i: t_part.at[i, 1], t_tmp, t_two, y, y_up, y_down
    )
    g_sum = [
        Scatter(
            lambda i, j=j: g_part.at[j, i], lambda i, j=j: g_part.at[j, i, 0:256],
            lambda i, j=j: g_part.at[j, i, 256:512], g_tmp.at[j], g_two.at[j], z, z_up, z_down,
        )
        for j in range(2)
    ]
    o_sum = [
        Scatter(
            lambda i, c=c: o_part.at[c, i], lambda i, c=c: o_part.at[c, i, 0:128],
            lambda i, c=c: o_part.at[c, i, 128:256], o_tmp.at[c], o_two.at[c], z, z_up, z_down,
        )
        for c in range(2)
    ]

    def t_dots(d, kk, dst):
        for half in range(2):
            dst[d, half] = dot(act[...].reshape(512, 512), ei[d, half * 2 + kk], ((1,), (0,))).astype(dst.dtype)

    def t_join(d):
        arrived(t_sib_in.at[d], t1 + d)
        for half in range(2):
            t_part[ring(y, d), half] = (t_own[d, half] + t_sib_in[d, half].astype(F32)).astype(BF16)

    act_copy.wait()
    for d in order:
        for copy in ei_copies(d):
            copy.wait()
    t_dots(2, 1 - k, t_sib)
    a_own_copy.wait()
    pl.semaphore_wait(barrier, expected)
    send(t_sib.at[2], t_sib_in.at[2], sib, t1 + 2)
    spread_send()
    c1_send(0)
    c2_send(0, 0)
    a_ring[0].start()
    a1_send()
    t_dots(2, k, t_own)
    for d in order[1:]:
        t_dots(d, 1 - k, t_sib)
        send(t_sib.at[d], t_sib_in.at[d], sib, t1 + d)
    t_join(2)
    t_sum.start()
    for d in order[1:]:
        t_dots(d, k, t_own)
    for d in order[1:]:
        t_join(d)
    for n in range(2):
        arrived(c_spread.at[:, n * 64:n * 64 + 64], sp + n)
    c1_send(1)
    c2_send(0, 1)
    arrived(c1_in.at[0], c1)
    c2_send(1, 0)
    s1_send()
    t_sum.pass_up()
    t_sum.pass_down()

    def c_enter(j):
        for i in range(4):
            arrived(c_all.at[k, j, y, i], c2r[j] + i)
        c_ring[j].start()
        send(c_all.at[k, j, y], c_all.at[k, j, y], sib, c4[j])

    def c_pass(j):
        c_ring[j].pass_up()
        c_ring[j].pass_down()
        for n, d in ((1, 3), (2, 1)):
            send(c_all.at[k, j, ring(y, d)], c_all.at[k, j, ring(y, d)], sib, c4[j] + n)

    def c_finish(j):
        c_ring[j].finish()
        for n, half in ((3, slice(0, 2)), (4, slice(2, 4))):
            send(c_all.at[k, j, ring(y, 2), half], c_all.at[k, j, ring(y, 2), half], sib, c4[j] + n)

    def c_sibling(j):
        for n, d in ((0, 0), (1, 3), (2, 1)):
            arrived(c_all.at[1 - k, j, ring(y, d)], c4[j] + n)
        for n, half in ((3, slice(0, 2)), (4, slice(2, 4))):
            arrived(c_all.at[1 - k, j, ring(y, 2), half], c4[j] + n)

    arrived(a_all.at[:, x, :, a_cols(1 - zh)], a1)
    a_ring[1].start()
    arrived(c1_in.at[1], c1 + 1)
    c2_send(1, 1)
    a_ring[0].pass_up()
    a_ring[0].pass_down()
    c_enter(0)

    def t_enter(c):
        rows = slice(c * 256, c * 256 + 256)
        arrived(t_swap_in.at[rows], t3 + c)
        t_all[y, rows] = (t_own[0, zh, rows] + t_swap_in[rows].astype(F32)).astype(BF16)
        t_ring[c].start()

    t_sum.finish()
    for c in range(2):
        rows = slice(c * 256, c * 256 + 256)
        for half in range(2):
            t_own[0, half, rows] = (
                t_part[y, half, rows].astype(F32)
                + t_two[0, half, rows].astype(F32)
                + t_two[1, half, rows].astype(F32)
            )
        t_swap[rows] = t_own[0, 1 - zh, rows].astype(BF16)
        send(t_swap.at[rows], t_swap_in.at[rows], z_far, t3 + c)
    e1_send()
    a_ring[1].pass_up()
    a_ring[1].pass_down()
    for i in range(8):
        arrived(s_home, s1 + i)
    s_ring.start()
    c_pass(0)
    c_enter(1)
    t_enter(0)
    t_enter(1)
    c_finish(0)
    for ring_of_a in a_ring:
        ring_of_a.finish()
    c_sibling(0)

    def g_block(j):
        @pl.loop(0, 4)
        def _(n):
            v, kk = n // 2, n % 2
            home = 2 * v + x1
            for half in range(2):
                cols = slice(half * 512, half * 512 + 512)
                total = dot(
                    c_all[kk, j, home].reshape(512, 256), a_all[0, :, :, cols].reshape(512, 512), ((0,), (0,))
                )
                for d, toks in ((1, slice(0, 64)), (3, slice(64, 128))):
                    total += dot(
                        c_all[kk, j, ring(home, d), :, toks].reshape(256, 256),
                        a_all[1, :, toks, cols].reshape(256, 512), ((0,), (0,)),
                    )
                g_part[j, half * 2 + v, pl.ds(pl.multiple_of(kk * 256, 256), 256)] = total.astype(BF16)

    g_block(0)
    g_sum[0].start()
    t_ring[0].pass_up()
    t_ring[0].pass_down()
    c_pass(1)
    t_ring[1].pass_up()
    t_ring[1].pass_down()
    s_ring.pass_up()
    s_ring.pass_down()
    g_sum[0].pass_up()
    g_sum[0].pass_down()
    e2_send()
    c_finish(1)
    c_sibling(1)
    g_block(1)
    g_sum[1].start()

    def u_dot(c, n):
        total = None
        for i in range(4):
            part = dot(
                t_all[i, c * 256:c * 256 + 256], s_all[n // 4, n % 4, :, i * 256:(i + 1) * 256], ((1,), (1,))
            )
            total = part if total is None else total + part
        return total

    for c in range(2):
        t_ring[c].finish()
        if c == 0:
            s_ring.finish()
        for n in range(8):
            u_own[c, n % 2, n // 2] = u_dot(c, n)
        u_sib[c] = u_own[c, 1 - k].astype(BF16)
        send(u_sib.at[c], u_sib_in.at[c], sib, u1 + c)
    for c in range(2):
        arrived(u_sib_in.at[c], u1 + c)
        u_part[c] = (u_own[c, k] + u_sib_in[c].astype(F32)).astype(BF16)
        for d in (1, 3, 2):
            send(u_part.at[c, ring(z, d)], u_in.at[c, d], at(z=ring(z, d)), u2[c] + d)
    e_enter()

    def u_enter(c):
        rows = slice(c * 256, c * 256 + 256)
        for d in (1, 3, 2):
            arrived(u_in.at[c, d], u2[c] + d)
        u_all[zl, rows, u_cols(k, y)] = (u_part[c, z].astype(F32) + u_in[c, 2].astype(F32)).astype(BF16)
        u_all[1 - zl, rows, u_cols(k, y)] = (u_in[c, 1].astype(F32) + u_in[c, 3].astype(F32)).astype(BF16)
        u_ring[c].start()
        send(u_block(c, k, y), u_block(c, k, y), sib, u4[c])

    def u_pass(c):
        u_ring[c].pass_up()
        u_ring[c].pass_down()
        for n, d in ((1, 3), (2, 1)):
            send(u_block(c, k, ring(y, d)), u_block(c, k, ring(y, d)), sib, u4[c] + n)

    def u_finish(c):
        u_ring[c].finish()
        for n in range(2):
            half = u_block(c, k, ring(y, 2), n)
            send(half, half, sib, u4[c] + 3 + n)
        for n, d in ((0, 0), (1, 3), (2, 1)):
            arrived(u_block(c, 1 - k, ring(y, d)), u4[c] + n)
        for n in range(2):
            arrived(u_block(c, 1 - k, ring(y, 2), n), u4[c] + 3 + n)

    u_enter(0)
    u_enter(1)
    g_sum[1].pass_up()
    g_sum[1].pass_down()
    e_ring.pass_up()
    e_ring.pass_down()
    u_pass(0)
    u_pass(1)
    u_finish(0)
    e_ring.finish()

    def o_block(c):
        for v in range(2):
            for w in range(2):
                slot = 2 * y0 + v
                if w:
                    slot = outer(slot)
                weight = e_all[slot].reshape(256, 1024)
                for tok in range(2):
                    total = dot(u_all[tok, c * 256:c * 256 + 256], weight, ((1,), (1,))).astype(BF16)
                    for n in range(2):
                        o_part[c, v * 2 + tok, :, n * 256 + w * 128:n * 256 + w * 128 + 128] = total[
                            :, n * 128:n * 128 + 128
                        ]

    o_block(0)
    o_sum[0].start()
    u_finish(1)
    o_block(1)
    o_sum[1].start()
    g_sum[0].finish()
    o_sum[0].pass_up()
    o_sum[0].pass_down()
    o_sum[1].pass_up()
    o_sum[1].pass_down()

    def last(dst, part, two, first, to):
        @pl.loop(0, 4)
        def _(i):
            src = pl.ds(pl.multiple_of(first + i * 64, 64), 64)
            dst[pl.ds(pl.multiple_of(to + i * 64, 64), 64)] = (
                part[src].astype(F32) + two[0, src].astype(F32) + two[1, src].astype(F32)
            ).astype(BF16)

    g_sum[1].finish()
    for j in range(2):
        for kk in range(2):
            last(grad_v, g_part.at[j, z], g_two.at[j], kk * 256, kk * 512 + j * 256)
    writes = [pltpu.make_async_copy(grad_v, grad_ref, out_sem.at[0])]
    writes[0].start()
    for c in range(2):
        o_sum[c].finish()
        rows = slice(c * 256, c * 256 + 256)
        last(out_v, o_part.at[c, z], o_two.at[c], 0, c * 256)
        writes.append(pltpu.make_async_copy(out_v.at[rows], out_ref.at[rows], out_sem.at[1 + c]))
        writes[-1].start()
    for copy, when in sent:
        if when is None:
            copy.wait_send()
        else:
            pl.when(when)(copy.wait_send)
    for copy in writes:
        copy.wait()


def place(out_in, grad_in, out_ref, grad_ref, rows, in_sem, out_sem):
    parts = [(out_in, out_ref, i) for i in range(2)] + [(grad_in, grad_ref, i) for i in range(4)]
    reads, writes = [], []
    for n, (src, dst, i) in enumerate(parts):
        part = pl.ds(i * 256, 256)
        reads.append(pltpu.make_async_copy(src.at[part], rows.at[n], in_sem.at[n]))
        writes.append(pltpu.make_async_copy(rows.at[n], dst.at[part], out_sem.at[n]))
        reads[n].start()
    for read, write in zip(reads, writes):
        read.wait()
        write.start()
    for write in writes:
        write.wait()


def per_device(small_weight, expand_out, expand_in, activations, cotangent):
    hbm = pl.BlockSpec(memory_space=pl.ANY)

    def buf(*shape, dtype=BF16):
        return pltpu.VMEM(shape, dtype)

    out, grad = pl.pallas_call(
        kernel,
        out_shape=(
            jax.ShapeDtypeStruct((512, 512), BF16),
            jax.ShapeDtypeStruct((1024, 512), BF16),
        ),
        in_specs=[hbm] * 5,
        out_specs=(hbm, hbm),
        scratch_shapes=[
            buf(4, 4, 512, 256),
            buf(2, 2, 128, 512),
            pltpu.SemaphoreType.DMA((18,)),
            buf(2, 4, 128, 1024),
            buf(4, 64, 1024),
            buf(4, 4, 64, 1024),
            buf(512, 512),
            buf(1024, 512),
            pltpu.SemaphoreType.DMA((3,)),
            buf(2, 4, 128, 1024),
            buf(2, 2, 4, 4, 128, 256),
            buf(2, 128, 512),
            buf(2, 128, 512),
            buf(4, 2, 512, 256),
            buf(4, 2, 512, 256),
            buf(4, 2, 512, 256, dtype=F32),
            buf(4, 2, 512, 256),
            buf(2, 512, 256),
            buf(2, 2, 512, 256),
            buf(512, 256),
            buf(512, 256),
            buf(4, 512, 256),
            buf(2, 2, 4, 256, 128, dtype=F32),
            buf(2, 4, 256, 128),
            buf(2, 4, 256, 128),
            buf(2, 4, 256, 128),
            buf(2, 4, 256, 128),
            buf(2, 512, 1024),
            buf(2, 4, 256, 512),
            buf(2, 2, 128, 512),
            buf(2, 2, 256, 512),
            buf(2, 4, 512, 512),
            buf(2, 2, 256, 512),
            buf(2, 2, 512, 512),
            pltpu.SemaphoreType.DMA((N_SEM,)),
            pltpu.SemaphoreType.DMA((N_SEM,)),
        ],
        compiler_params=pltpu.CompilerParams(
            collective_id=0, has_side_effects=True, vmem_limit_bytes=58 * 2**20
        ),
        cost_estimate=pl.CostEstimate(flops=9_700_000_000, bytes_accessed=8_000_000, transcendentals=0),
        name="grow",
    )(
        small_weight,
        expand_out,
        expand_in,
        activations.reshape(2, 2, 128, 512),
        cotangent.reshape(2, 2, 128, 512),
    )
    return pl.pallas_call(
        place,
        out_shape=(jax.ShapeDtypeStruct(out.shape, BF16), jax.ShapeDtypeStruct(grad.shape, BF16)),
        in_specs=[hbm] * 2,
        out_specs=(hbm, hbm),
        scratch_shapes=[buf(6, 256, 512), pltpu.SemaphoreType.DMA((6,)), pltpu.SemaphoreType.DMA((6,))],
        name="place",
    )(out, grad)


def solution(mesh):
    in_specs = (
        P(("row", "col"), None),
        P(("row", "col"), None),
        P("col", None),
        P("row", "col"),
        P("row", "col"),
    )
    out_specs = (P("row", "col"), P("row", "col"))
    return jax.shard_map(per_device, mesh=mesh, in_specs=in_specs, out_specs=out_specs, check_vma=False)
```

```python
import math

import jax
import jax.numpy as jnp
from jax import lax
from jax.experimental import pallas as pl
from jax.experimental.pallas import tpu as pltpu
from jax.sharding import PartitionSpec as P

MESH = pl.DeviceIdType.MESH
F32 = jnp.float32
BF16 = jnp.bfloat16
N_RECV, N_SEND, LONE = 92, 14, 8
GROUP = 4 * 2**20
PARTS = 4
WIDE = 512 // PARTS


def dot(a, b, dims):
    return lax.dot_general(a, b, (dims, ((), ())), preferred_element_type=F32)


def kernel(
    sw, eo, ei_hbm, act_hbm, cot, out_ref, grad_ref,
    ei, act, in_sem, s_all, e_z, e_all, out_v, grad_v, out_sem, a_all, c_all, c_spread, c1_in,
    t_sib, t_sib_in, t_own, t_part, t_tmp, t_two, t_swap, t_swap_in, t_all,
    u_own, u_sib, u_sib_in, u_part, u_in, u_all,
    o_part, o_tmp, o_two, g_part, g_tmp, g_two,
    ssem, rsem,
):
    row, col = lax.axis_index("row"), lax.axis_index("col")
    x, zl = row % 4, row // 4
    k, zh, y = col % 2, (col // 2) % 2, col // 4
    z = zh * 2 + zl
    y0, y1, x0, x1 = y % 2, y // 2, x % 2, x // 2

    def at(x=x, y=y, z=z, k=k):
        return ((z % 2) * 4 + x, (y * 2 + z // 2) * 2 + k)

    def ring(i, d):
        return (i + d) % 4

    def outer(i):
        return ring(i, 3 + 2 * (i % 2))

    sib = at(k=1 - k)
    x_up, x_down = at(x=ring(x, 1)), at(x=ring(x, 3))
    y_up, y_down = at(y=ring(y, 1)), at(y=ring(y, 3))
    z_up, z_down = at(z=ring(z, 1)), at(z=ring(z, 3))
    z_far = at(z=ring(z, 2))

    c_x = [[2 * y0 + zh, 2 * (1 - y0) + zh], [2 * y0 + 1 - zh, 2 * (1 - y0) + 1 - zh]]
    c_home = x1 == y0
    e_x = [x, x, outer(x), outer(x)]
    e_to = [at(x=e_x[i], y=(i % 2) * 2 + x1, k=y1) for i in range(4)]
    e_src_x = jnp.where(c_home, x, outer(x))

    order = (2, 1, 3, 0)
    act_copy = pltpu.make_async_copy(act_hbm, act, in_sem.at[16])
    act_copy.start()

    def ei_copies(d):
        return [
            pltpu.make_async_copy(
                ei_hbm.at[:, pl.ds(pl.multiple_of(q * 1024 + ring(y, d) * 256, 256), 256)], ei.at[d, q], in_sem.at[d * 4 + q]
            )
            for q in range(4)
        ]

    def a_cols(half):
        return pl.ds(pl.multiple_of(half * 512, 512), 512)

    a_own_copy = pltpu.make_async_copy(act_hbm.at[zh], a_all.at[:, x, :, a_cols(zh)], in_sem.at[17])
    a_own_copy.start()
    for d in order:
        for copy in ei_copies(d):
            copy.start()

    barrier = pltpu.get_barrier_semaphore()

    def greet(to):
        pl.semaphore_signal(barrier, inc=1, device_id=to, device_id_type=MESH)

    expected = 0
    for dz in range(4):
        for dk in range(2):
            if dz or dk:
                greet(at(z=ring(z, dz), k=(k + dk) % 2))
                expected += 1
    for to in (x_up, x_down, y_up, y_down):
        greet(to)
        expected += 1

    def greet_unless_self(to):
        other = jnp.logical_or(to[0] != row, to[1] != col)

        @pl.when(other)
        def _():
            greet(to)

        return other.astype(jnp.int32)

    for d in (2,):
        greet(at(x=ring(x, d)))
        expected += 1
    for to in e_to:
        expected += greet_unless_self(to)
    for i in range(4):
        expected += greet_unless_self(at(x=e_src_x, y=2 * k + i // 2, k=i % 2))
    count = [0]
    loads = [0]
    lone = []

    def ids(n):
        first = count[0]
        count[0] += n
        assert count[0] <= N_RECV
        return first

    def remote(src, dst, to, s, r):
        return pltpu.make_async_remote_copy(
            src_ref=src, dst_ref=dst, send_sem=ssem.at[s], recv_sem=rsem.at[r],
            device_id=to, device_id_type=MESH,
        )

    def send(src, dst, to, r):
        size = 2 * math.prod(src.shape)
        if loads[-1] + size > GROUP:
            loads.append(0)
        loads[-1] += size
        remote(src, dst, to, LONE + len(loads) - 1, r).start()

    def send_or_copy(src, dst, to, r):
        mine = jnp.logical_and(to[0] == row, to[1] == col)
        copy = remote(src, dst, to, len(lone), r)

        @pl.when(mine)
        def _():
            pltpu.make_async_copy(src, dst, rsem.at[r]).start()

        @pl.when(jnp.logical_not(mine))
        def _():
            copy.start()

        lone.append((copy, jnp.logical_not(mine)))

    def arrived(ref, r):
        remote(ref, ref, sib, 0, r).wait_recv()

    class Gather:
        def __init__(self, slot, first, second, me, up, down):
            self.slot, self.first, self.second, self.me = slot, first, second, me
            self.up, self.down, self.s = up, down, ids(3)

        def start(self):
            mine = self.slot(self.me)
            send(mine, mine, self.up, self.s)
            send(mine, mine, self.down, self.s + 1)

        def pass_up(self):
            i = ring(self.me, 3)
            arrived(self.slot(i), self.s)
            send(self.first(i), self.first(i), self.up, self.s + 2)

        def pass_down(self):
            i = ring(self.me, 1)
            arrived(self.slot(i), self.s + 1)
            send(self.second(i), self.second(i), self.down, self.s + 2)

        def finish(self):
            arrived(self.slot(ring(self.me, 2)), self.s + 2)

    class Scatter:
        def __init__(self, slot, first, second, tmp, two, me, up, down):
            self.slot, self.first, self.second = slot, first, second
            self.tmp, self.two, self.me, self.up, self.down, self.s = tmp, two, me, up, down, ids(3)

        def start(self):
            i = ring(self.me, 2)
            send(self.first(i), self.tmp.at[0], self.up, self.s)
            send(self.second(i), self.tmp.at[1], self.down, self.s + 1)

        def pass_up(self):
            i = ring(self.me, 1)
            arrived(self.tmp.at[0], self.s)
            add_into(self.first(i), self.tmp.at[0])
            send(self.slot(i), self.two.at[0], self.up, self.s + 2)

        def pass_down(self):
            i = ring(self.me, 3)
            arrived(self.tmp.at[1], self.s + 1)
            add_into(self.second(i), self.tmp.at[1])
            send(self.slot(i), self.two.at[1], self.down, self.s + 2)

        def finish(self):
            arrived(self.two, self.s + 2)

    def add_into(dst, src):
        rows = dst.shape[0]

        @pl.loop(0, rows // 64)
        def _(i):
            part = pl.ds(pl.multiple_of(i * 64, 64), 64)
            dst[part] = (dst[part].astype(F32) + src[part].astype(F32)).astype(BF16)

    sp, c1, a1, s1, e1, e2, c2 = ids(1), ids(2), ids(1), ids(1), ids(1), ids(1), ids(1)
    t1, t3, u1 = ids(4), ids(2), ids(2)
    u2, u4 = ids(2), ids(2)
    c4 = ids(PARTS)
    s_home = s_all.at[zl, x, pl.ds(pl.multiple_of(zh * 64 + k * 32, 32), 32)]

    def spread_send():
        for n, to in enumerate((y_up, y_down)):
            send(cot.at[:, 1, n * 64:n * 64 + 64], c_spread.at[:, n * 64:n * 64 + 64], to, sp)

    def c1_send(half):
        src = cot.at[1 - zh, 0] if half == 0 else c_spread.at[1 - zh]
        send(src, c1_in.at[half], z_far, c1 + half)

    def a1_send():
        send(act_hbm.at[1 - zh], a_all.at[:, x, :, a_cols(zh)], z_far, a1)

    def c2_send(other, half):
        if other:
            src = c1_in.at[half]
        else:
            src = c_spread.at[zh] if half else cot.at[zh, 0]
        send_or_copy(src, c_all.at[k, y, x], at(x=c_x[other][half]), c2)

    def s1_send():
        for dz in (1, 3, 2, 0):
            for dk in range(2):
                tz, tk = ring(z, dz), (k + dk) % 2
                piece = sw.at[:, pl.ds(pl.multiple_of(((tz // 2) * 2 + tk) * 1024, 1024), 1024)]
                if dz or dk:
                    send(piece, s_home, at(z=tz, k=tk), s1)
                else:
                    pltpu.make_async_copy(piece, s_home, rsem.at[s1]).start()

    def e1_send():
        for d in (1, 3, 2, 0):
            i = ring(z, d)
            piece = eo.at[:, pl.ds(pl.multiple_of(i * 1024, 1024), 1024)]
            if d:
                send(piece, e_z.at[z], at(z=i), e1)
            else:
                pltpu.make_async_copy(piece, e_z.at[z], rsem.at[e1]).start()

    def e2_send():
        arrived(e_z, e1)
        for i in range(4):
            send_or_copy(e_z.at[i], e_all.at[e_x[i], y0 * 2 + k], e_to[i], e2)

    def e_enter():
        arrived(e_all.at[x], e2)
        e_ring.start()

    s_ring = Gather(lambda i: s_all.at[:, i], lambda i: s_all.at[0, i], lambda i: s_all.at[1, i], x, x_up, x_down)
    a_ring = [
        Gather(
            lambda i, c=c: a_all.at[:, i, :, c], lambda i, c=c: a_all.at[0, i, :, c],
            lambda i, c=c: a_all.at[1, i, :, c], x, x_up, x_down,
        )
        for c in (a_cols(zh), a_cols(1 - zh))
    ]
    e_ring = Gather(
        lambda i: e_all.at[i], lambda i: e_all.at[i, 0:2], lambda i: e_all.at[i, 2:4], x, x_up, x_down
    )
    def c_block(kk, j, i, part=slice(None), toks=slice(None)):
        return c_all.at[kk, i, part, toks, j * WIDE:(j + 1) * WIDE]

    c_ring = [
        Gather(
            lambda i, j=j: c_block(k, j, i), lambda i, j=j: c_block(k, j, i, slice(0, 2)),
            lambda i, j=j: c_block(k, j, i, slice(2, 4)), y, y_up, y_down,
        )
        for j in range(PARTS)
    ]
    t_ring = [
        Gather(
            lambda i, c=c: t_all.at[i, c * 256:c * 256 + 256], lambda i, c=c: t_all.at[i, c * 256:c * 256 + 128],
            lambda i, c=c: t_all.at[i, c * 256 + 128:c * 256 + 256], y, y_up, y_down,
        )
        for c in range(2)
    ]

    def u_cols(kk, i):
        return pl.ds(pl.multiple_of(kk * 512 + i * 128, 128), 128)

    def u_block(c, kk, i, tok=slice(None)):
        return u_all.at[tok, c * 256:c * 256 + 256, u_cols(kk, i)]

    u_ring = [
        Gather(
            lambda i, c=c: u_block(c, k, i), lambda i, c=c: u_block(c, k, i, 0), lambda i, c=c: u_block(c, k, i, 1),
            y, y_up, y_down,
        )
        for c in range(2)
    ]
    t_sum = Scatter(
        lambda i: t_part.at[i], lambda i: t_part.at[i, 0], lambda i: t_part.at[i, 1], t_tmp, t_two, y, y_up, y_down
    )
    g_sum = [
        Scatter(
            lambda i, j=j: g_part.at[j, i], lambda i, j=j: g_part.at[j, i, 0:WIDE],
            lambda i, j=j: g_part.at[j, i, WIDE:2 * WIDE], g_tmp.at[j], g_two.at[j], z, z_up, z_down,
        )
        for j in range(PARTS)
    ]
    o_sum = [
        Scatter(
            lambda i, c=c: o_part.at[c, i], lambda i, c=c: o_part.at[c, i, 0:128],
            lambda i, c=c: o_part.at[c, i, 128:256], o_tmp.at[c], o_two.at[c], z, z_up, z_down,
        )
        for c in range(2)
    ]

    def t_dots(d, kk, dst):
        for half in range(2):
            dst[d, half] = dot(act[...].reshape(512, 512), ei[d, half * 2 + kk], ((1,), (0,))).astype(dst.dtype)

    def t_join(d):
        arrived(t_sib_in.at[d], t1 + d)
        for half in range(2):
            t_part[ring(y, d), half] = (t_own[d, half] + t_sib_in[d, half].astype(F32)).astype(BF16)

    act_copy.wait()
    for d in order:
        for copy in ei_copies(d):
            copy.wait()
    t_dots(2, 1 - k, t_sib)
    a_own_copy.wait()
    pl.semaphore_wait(barrier, expected)
    send(t_sib.at[2], t_sib_in.at[2], sib, t1 + 2)
    spread_send()
    c1_send(0)
    c2_send(0, 0)
    a_ring[0].start()
    a1_send()
    t_dots(2, k, t_own)
    for d in order[1:]:
        t_dots(d, 1 - k, t_sib)
        send(t_sib.at[d], t_sib_in.at[d], sib, t1 + d)
    t_join(2)
    t_sum.start()
    for d in order[1:]:
        t_dots(d, k, t_own)
    for d in order[1:]:
        t_join(d)
    arrived(c_spread, sp)
    c1_send(1)
    c2_send(0, 1)
    arrived(c1_in.at[0], c1)
    c2_send(1, 0)
    t_sum.pass_up()
    t_sum.pass_down()
    arrived(c1_in.at[1], c1 + 1)
    c2_send(1, 1)
    s1_send()
    e1_send()

    def c_enter(j):
        if j == 0:
            arrived(c_all.at[k, y], c2)
        c_ring[j].start()
        send(c_block(k, j, y), c_block(k, j, y), sib, c4 + j)

    def c_pass(j):
        c_ring[j].pass_up()
        c_ring[j].pass_down()
        for d in (3, 1):
            send(c_block(k, j, ring(y, d)), c_block(k, j, ring(y, d)), sib, c4 + j)

    def c_finish(j):
        c_ring[j].finish()
        for half in (slice(0, 2), slice(2, 4)):
            send(c_block(k, j, ring(y, 2), half), c_block(k, j, ring(y, 2), half), sib, c4 + j)

    def c_sibling(j):
        arrived(c_all.at[1 - k, :, :, :, j * WIDE:(j + 1) * WIDE], c4 + j)

    def t_enter(c):
        rows = slice(c * 256, c * 256 + 256)
        arrived(t_swap_in.at[rows], t3 + c)
        t_all[y, rows] = (t_own[0, zh, rows] + t_swap_in[rows].astype(F32)).astype(BF16)
        t_ring[c].start()

    def g_block(j):
        parts = (
            (0, slice(None), a_all.at[0]),
            (1, slice(0, 64), a_all.at[1, :, 0:64]),
            (3, slice(64, 128), a_all.at[1, :, 64:128]),
        )
        for half in range(2):
            total = None
            for d, toks, acts in parts:
                block = jnp.concatenate(
                    [
                        c_block(kk, j, ring(2 * v + x1, d), toks=toks)[...].reshape(-1, WIDE)
                        for v in range(2)
                        for kk in range(2)
                    ],
                    axis=1,
                )
                part = dot(block, acts[:, :, half * 512:half * 512 + 512].reshape(-1, 512), ((0,), (0,)))
                total = part if total is None else total + part
            total = total.astype(BF16)
            for v in range(2):
                g_part[j, half * 2 + v] = total[v * 2 * WIDE:(v + 1) * 2 * WIDE]

    def g_enter(j):
        c_sibling(j)
        g_block(j)
        g_sum[j].start()

    def g_pass(j):
        g_sum[j].pass_up()
        g_sum[j].pass_down()

    def t_leave():
        t_sum.finish()
        for c in range(2):
            rows = slice(c * 256, c * 256 + 256)
            for half in range(2):
                t_own[0, half, rows] = (
                    t_part[y, half, rows].astype(F32)
                    + t_two[0, half, rows].astype(F32)
                    + t_two[1, half, rows].astype(F32)
                )
            t_swap[rows] = t_own[0, 1 - zh, rows].astype(BF16)
            send(t_swap.at[rows], t_swap_in.at[rows], z_far, t3 + c)

    def t_pass():
        for c in range(2):
            t_ring[c].pass_up()
            t_ring[c].pass_down()

    def both(gather):
        gather.pass_up()
        gather.pass_down()

    arrived(a_all.at[:, x, :, a_cols(1 - zh)], a1)
    a_ring[1].start()
    both(a_ring[0])
    c_enter(0)
    both(a_ring[1])
    t_leave()
    c_pass(0)
    c_enter(1)
    c_enter(2)
    arrived(s_all.at[:, x], s1)
    s_ring.start()
    c_finish(0)
    for ring_of_a in a_ring:
        ring_of_a.finish()
    g_enter(0)
    c_pass(1)
    t_enter(0)
    t_enter(1)
    c_pass(2)
    g_pass(0)
    c_finish(1)
    g_enter(1)
    t_pass()
    c_enter(3)
    both(s_ring)
    e2_send()
    g_pass(1)

    def u_dot(c, n):
        total = None
        for i in range(4):
            part = dot(
                t_all[i, c * 256:c * 256 + 256], s_all[n // 4, n % 4, :, i * 256:(i + 1) * 256], ((1,), (1,))
            )
            total = part if total is None else total + part
        return total

    for c in range(2):
        t_ring[c].finish()
        if c == 0:
            s_ring.finish()
        for n in range(8):
            u_own[c, n % 2, n // 2] = u_dot(c, n)
        u_sib[c] = u_own[c, 1 - k].astype(BF16)
        send(u_sib.at[c], u_sib_in.at[c], sib, u1 + c)
    for c in range(2):
        arrived(u_sib_in.at[c], u1 + c)
        u_part[c] = (u_own[c, k] + u_sib_in[c].astype(F32)).astype(BF16)
        for d in (1, 3, 2):
            send(u_part.at[c, ring(z, d)], u_in.at[c, d], at(z=ring(z, d)), u2 + c)
    e_enter()
    c_finish(2)
    g_enter(2)
    c_pass(3)

    def u_enter(c):
        rows = slice(c * 256, c * 256 + 256)
        arrived(u_in.at[c, 1:4], u2 + c)
        u_all[zl, rows, u_cols(k, y)] = (u_part[c, z].astype(F32) + u_in[c, 2].astype(F32)).astype(BF16)
        u_all[1 - zl, rows, u_cols(k, y)] = (u_in[c, 1].astype(F32) + u_in[c, 3].astype(F32)).astype(BF16)
        u_ring[c].start()
        send(u_block(c, k, y), u_block(c, k, y), sib, u4 + c)

    def u_pass(c):
        u_ring[c].pass_up()
        u_ring[c].pass_down()
        for d in (3, 1):
            send(u_block(c, k, ring(y, d)), u_block(c, k, ring(y, d)), sib, u4 + c)

    def u_finish(c):
        u_ring[c].finish()
        for n in range(2):
            half = u_block(c, k, ring(y, 2), n)
            send(half, half, sib, u4 + c)
        arrived(u_all.at[:, c * 256:c * 256 + 256, pl.ds(pl.multiple_of((1 - k) * 512, 512), 512)], u4 + c)

    u_enter(0)
    u_enter(1)
    g_pass(2)
    c_finish(3)
    g_enter(3)
    both(e_ring)
    u_pass(0)
    u_pass(1)
    g_pass(3)
    u_finish(0)
    e_ring.finish()

    def o_block(c):
        for v in range(2):
            for w in range(2):
                slot = 2 * y0 + v
                if w:
                    slot = outer(slot)
                weight = e_all[slot].reshape(256, 1024)
                for tok in range(2):
                    total = dot(u_all[tok, c * 256:c * 256 + 256], weight, ((1,), (1,))).astype(BF16)
                    for n in range(2):
                        o_part[c, v * 2 + tok, :, n * 256 + w * 128:n * 256 + w * 128 + 128] = total[
                            :, n * 128:n * 128 + 128
                        ]

    o_block(0)
    o_sum[0].start()
    u_finish(1)
    o_block(1)
    o_sum[1].start()
    o_sum[0].pass_up()
    o_sum[0].pass_down()
    o_sum[1].pass_up()
    o_sum[1].pass_down()

    def last(dst, part, two, rows, first, to):
        @pl.loop(0, rows // 64)
        def _(i):
            src = pl.ds(pl.multiple_of(first + i * 64, 64), 64)
            dst[pl.ds(pl.multiple_of(to + i * 64, 64), 64)] = (
                part[src].astype(F32) + two[0, src].astype(F32) + two[1, src].astype(F32)
            ).astype(BF16)

    for j in range(PARTS):
        g_sum[j].finish()
        for kk in range(2):
            last(grad_v, g_part.at[j, z], g_two.at[j], WIDE, kk * WIDE, kk * 512 + j * WIDE)
    writes = [pltpu.make_async_copy(grad_v, grad_ref, out_sem.at[0])]
    writes[0].start()
    for c in range(2):
        o_sum[c].finish()
        rows = slice(c * 256, c * 256 + 256)
        last(out_v, o_part.at[c, z], o_two.at[c], 256, 0, c * 256)
        writes.append(pltpu.make_async_copy(out_v.at[rows], out_ref.at[rows], out_sem.at[1 + c]))
        writes[-1].start()
    assert len(lone) <= LONE and len(loads) <= N_SEND - LONE
    for copy, when in lone:
        pl.when(when)(copy.wait_send)
    for n, size in enumerate(loads):
        rows = ei_hbm.at[0:size // 8192]
        remote(rows, rows, sib, LONE + n, 0).wait_send()
    for copy in writes:
        copy.wait()


def place(out_in, grad_in, out_ref, grad_ref, rows, in_sem, out_sem):
    parts = [(out_in, out_ref, i) for i in range(2)] + [(grad_in, grad_ref, i) for i in range(4)]
    reads, writes = [], []
    for n, (src, dst, i) in enumerate(parts):
        part = pl.ds(i * 256, 256)
        reads.append(pltpu.make_async_copy(src.at[part], rows.at[n], in_sem.at[n]))
        writes.append(pltpu.make_async_copy(rows.at[n], dst.at[part], out_sem.at[n]))
        reads[n].start()
    for read, write in zip(reads, writes):
        read.wait()
        write.start()
    for write in writes:
        write.wait()


def per_device(small_weight, expand_out, expand_in, activations, cotangent):
    hbm = pl.BlockSpec(memory_space=pl.ANY)

    def buf(*shape, dtype=BF16):
        return pltpu.VMEM(shape, dtype)

    out, grad = pl.pallas_call(
        kernel,
        out_shape=(
            jax.ShapeDtypeStruct((512, 512), BF16),
            jax.ShapeDtypeStruct((1024, 512), BF16),
        ),
        in_specs=[hbm] * 5,
        out_specs=(hbm, hbm),
        scratch_shapes=[
            buf(4, 4, 512, 256),
            buf(2, 2, 128, 512),
            pltpu.SemaphoreType.DMA((18,)),
            buf(2, 4, 128, 1024),
            buf(4, 64, 1024),
            buf(4, 4, 64, 1024),
            buf(512, 512),
            buf(1024, 512),
            pltpu.SemaphoreType.DMA((3,)),
            buf(2, 4, 128, 1024),
            buf(2, 4, 4, 128, 512),
            buf(2, 128, 512),
            buf(2, 128, 512),
            buf(4, 2, 512, 256),
            buf(4, 2, 512, 256),
            buf(4, 2, 512, 256, dtype=F32),
            buf(4, 2, 512, 256),
            buf(2, 512, 256),
            buf(2, 2, 512, 256),
            buf(512, 256),
            buf(512, 256),
            buf(4, 512, 256),
            buf(2, 2, 4, 256, 128, dtype=F32),
            buf(2, 4, 256, 128),
            buf(2, 4, 256, 128),
            buf(2, 4, 256, 128),
            buf(2, 4, 256, 128),
            buf(2, 512, 1024),
            buf(2, 4, 256, 512),
            buf(2, 2, 128, 512),
            buf(2, 2, 256, 512),
            buf(PARTS, 4, 2 * WIDE, 512),
            buf(PARTS, 2, WIDE, 512),
            buf(PARTS, 2, 2 * WIDE, 512),
            pltpu.SemaphoreType.DMA((N_SEND,)),
            pltpu.SemaphoreType.DMA((N_RECV,)),
        ],
        compiler_params=pltpu.CompilerParams(
            collective_id=0, has_side_effects=True, vmem_limit_bytes=58 * 2**20
        ),
        cost_estimate=pl.CostEstimate(flops=9_700_000_000, bytes_accessed=8_000_000, transcendentals=0),
        name="grow",
    )(
        small_weight,
        expand_out,
        expand_in,
        activations.reshape(2, 2, 128, 512),
        cotangent.reshape(2, 2, 128, 512),
    )
    return pl.pallas_call(
        place,
        out_shape=(jax.ShapeDtypeStruct(out.shape, BF16), jax.ShapeDtypeStruct(grad.shape, BF16)),
        in_specs=[hbm] * 2,
        out_specs=(hbm, hbm),
        scratch_shapes=[buf(6, 256, 512), pltpu.SemaphoreType.DMA((6,)), pltpu.SemaphoreType.DMA((6,))],
        name="place",
    )(out, grad)


def solution(mesh):
    in_specs = (
        P(("row", "col"), None),
        P(("row", "col"), None),
        P("col", None),
        P("row", "col"),
        P("row", "col"),
    )
    out_specs = (P("row", "col"), P("row", "col"))
    return jax.shard_map(per_device, mesh=mesh, in_specs=in_specs, out_specs=out_specs, check_vma=False)
```

```python
import math

import jax
import jax.numpy as jnp
from jax import lax
from jax.experimental import pallas as pl
from jax.experimental.pallas import tpu as pltpu
from jax.sharding import PartitionSpec as P

MESH = pl.DeviceIdType.MESH
F32 = jnp.float32
BF16 = jnp.bfloat16
N_RECV, N_SEND, LONE = 96, 18, 12
GROUP = 4 * 2**20
PARTS = 4
WIDE = 512 // PARTS


def dot(a, b, dims):
    return lax.dot_general(a, b, (dims, ((), ())), preferred_element_type=F32)


def kernel(
    sw, eo, ei_hbm, act_hbm, cot, out_ref, grad_ref,
    ei, act, in_sem, s_all, e_z, e_all,  a_all, c_all, c_spread, c1_in,
    t_sib, t_sib_in, t_own, t_part, t_tmp, t_two, t_swap, t_swap_in, t_all,
    u_own, u_sib, u_sib_in, u_part, u_in, u_all,
    o_part, o_tmp, o_two, g_part, g_tmp, g_two,
    ssem, rsem,
):
    row, col = lax.axis_index("row"), lax.axis_index("col")
    x, zl = row % 4, row // 4
    k, zh, y = col % 2, (col // 2) % 2, col // 4
    z = zh * 2 + zl
    y0, y1, x0, x1 = y % 2, y // 2, x % 2, x // 2

    def at(x=x, y=y, z=z, k=k):
        return ((z % 2) * 4 + x, (y * 2 + z // 2) * 2 + k)

    def ring(i, d):
        return (i + d) % 4

    def outer(i):
        return ring(i, 3 + 2 * (i % 2))

    sib = at(k=1 - k)
    x_up, x_down = at(x=ring(x, 1)), at(x=ring(x, 3))
    y_up, y_down = at(y=ring(y, 1)), at(y=ring(y, 3))
    z_up, z_down = at(z=ring(z, 1)), at(z=ring(z, 3))
    z_far = at(z=ring(z, 2))

    c_x = [[2 * y0 + zh, 2 * (1 - y0) + zh], [2 * y0 + 1 - zh, 2 * (1 - y0) + 1 - zh]]
    c_home = x1 == y0
    e_x = [x, x, outer(x), outer(x)]
    e_to = [at(x=e_x[i], y=(i % 2) * 2 + x1, k=y1) for i in range(4)]
    e_src_x = jnp.where(c_home, x, outer(x))

    order = (2, 1, 3, 0)
    act_copy = pltpu.make_async_copy(act_hbm, act, in_sem.at[16])
    act_copy.start()

    def ei_copies(d):
        return [
            pltpu.make_async_copy(
                ei_hbm.at[:, pl.ds(pl.multiple_of(q * 1024 + ring(y, d) * 256, 256), 256)], ei.at[d, q], in_sem.at[d * 4 + q]
            )
            for q in range(4)
        ]

    def a_cols(half):
        return pl.ds(pl.multiple_of(half * 512, 512), 512)

    a_own_copy = pltpu.make_async_copy(act_hbm.at[zh], a_all.at[:, x, :, a_cols(zh)], in_sem.at[17])
    a_own_copy.start()
    for d in order:
        for copy in ei_copies(d):
            copy.start()

    barrier = pltpu.get_barrier_semaphore()

    def greet(to):
        pl.semaphore_signal(barrier, inc=1, device_id=to, device_id_type=MESH)

    expected = 0
    for dz in range(4):
        for dk in range(2):
            if dz or dk:
                greet(at(z=ring(z, dz), k=(k + dk) % 2))
                expected += 1
    for to in (x_up, x_down, y_up, y_down):
        greet(to)
        expected += 1

    def greet_unless_self(to):
        other = jnp.logical_or(to[0] != row, to[1] != col)

        @pl.when(other)
        def _():
            greet(to)

        return other.astype(jnp.int32)

    for d in (2,):
        greet(at(x=ring(x, d)))
        expected += 1
    for to in e_to:
        expected += greet_unless_self(to)
    for i in range(4):
        expected += greet_unless_self(at(x=e_src_x, y=2 * k + i // 2, k=i % 2))
    count = [0]
    loads = [0]
    lone = []

    def ids(n):
        first = count[0]
        count[0] += n
        assert count[0] <= N_RECV
        return first

    def remote(src, dst, to, s, r):
        return pltpu.make_async_remote_copy(
            src_ref=src, dst_ref=dst, send_sem=ssem.at[s], recv_sem=rsem.at[r],
            device_id=to, device_id_type=MESH,
        )

    def send(src, dst, to, r):
        size = 2 * math.prod(src.shape)
        if loads[-1] + size > GROUP:
            loads.append(0)
        loads[-1] += size
        remote(src, dst, to, LONE + len(loads) - 1, r).start()

    def send_or_copy(src, dst, to, r):
        mine = jnp.logical_and(to[0] == row, to[1] == col)
        copy = remote(src, dst, to, len(lone), r)

        @pl.when(mine)
        def _():
            pltpu.make_async_copy(src, dst, rsem.at[r]).start()

        @pl.when(jnp.logical_not(mine))
        def _():
            copy.start()

        lone.append((copy, jnp.logical_not(mine)))

    def arrived(ref, r):
        remote(ref, ref, sib, 0, r).wait_recv()

    class Gather:
        def __init__(self, slot, first, second, me, up, down):
            self.slot, self.first, self.second, self.me = slot, first, second, me
            self.up, self.down, self.s = up, down, ids(3)

        def start(self):
            mine = self.slot(self.me)
            send(mine, mine, self.up, self.s)
            send(mine, mine, self.down, self.s + 1)

        def pass_up(self):
            i = ring(self.me, 3)
            arrived(self.slot(i), self.s)
            send(self.first(i), self.first(i), self.up, self.s + 2)

        def pass_down(self):
            i = ring(self.me, 1)
            arrived(self.slot(i), self.s + 1)
            send(self.second(i), self.second(i), self.down, self.s + 2)

        def finish(self):
            arrived(self.slot(ring(self.me, 2)), self.s + 2)

    class Scatter:
        def __init__(self, slot, first, second, tmp, two, me, up, down):
            self.slot, self.first, self.second = slot, first, second
            self.tmp, self.two, self.me, self.up, self.down, self.s = tmp, two, me, up, down, ids(3)

        def start(self):
            i = ring(self.me, 2)
            send(self.first(i), self.tmp.at[0], self.up, self.s)
            send(self.second(i), self.tmp.at[1], self.down, self.s + 1)

        def pass_up(self):
            i = ring(self.me, 1)
            arrived(self.tmp.at[0], self.s)
            add_into(self.first(i), self.tmp.at[0])
            send(self.slot(i), self.two.at[0], self.up, self.s + 2)

        def pass_down(self):
            i = ring(self.me, 3)
            arrived(self.tmp.at[1], self.s + 1)
            add_into(self.second(i), self.tmp.at[1])
            send(self.slot(i), self.two.at[1], self.down, self.s + 2)

        def finish(self):
            arrived(self.two, self.s + 2)

    def add_into(dst, src):
        rows = dst.shape[0]

        @pl.loop(0, rows // 64)
        def _(i):
            part = pl.ds(pl.multiple_of(i * 64, 64), 64)
            dst[part] = (dst[part].astype(F32) + src[part].astype(F32)).astype(BF16)

    sp, c1, a1, s1, e1, e2, c2 = ids(1), ids(2), ids(1), ids(1), ids(1), ids(2), ids(1)
    t1, t3, u1 = ids(4), ids(2), ids(2)
    u2, u4 = ids(2), ids(2)
    c4 = ids(PARTS)
    s_home = s_all.at[zl, x, pl.ds(pl.multiple_of(zh * 64 + k * 32, 32), 32)]

    def spread_send():
        for n, to in enumerate((y_up, y_down)):
            send(cot.at[:, 1, n * 64:n * 64 + 64], c_spread.at[:, n * 64:n * 64 + 64], to, sp)

    def c1_send(half):
        src = cot.at[1 - zh, 0] if half == 0 else c_spread.at[1 - zh]
        send(src, c1_in.at[half], z_far, c1 + half)

    def a1_send():
        send(act_hbm.at[1 - zh], a_all.at[:, x, :, a_cols(zh)], z_far, a1)

    def c2_send(other, half):
        if other:
            src = c1_in.at[half]
        else:
            src = c_spread.at[zh] if half else cot.at[zh, 0]
        send_or_copy(src, c_all.at[k, y, x], at(x=c_x[other][half]), c2)

    def s1_send():
        for dz in (1, 3, 2, 0):
            for dk in range(2):
                tz, tk = ring(z, dz), (k + dk) % 2
                piece = sw.at[:, pl.ds(pl.multiple_of(((tz // 2) * 2 + tk) * 1024, 1024), 1024)]
                if dz or dk:
                    send(piece, s_home, at(z=tz, k=tk), s1)
                else:
                    pltpu.make_async_copy(piece, s_home, rsem.at[s1]).start()

    def e1_send():
        for d in (1, 3, 2, 0):
            i = ring(z, d)
            piece = eo.at[:, pl.ds(pl.multiple_of(i * 1024, 1024), 1024)]
            if d:
                send(piece, e_z.at[z], at(z=i), e1)
            else:
                pltpu.make_async_copy(piece, e_z.at[z], rsem.at[e1]).start()

    def e_cols(h):
        return slice(h * 512, h * 512 + 512)

    def e2_send():
        arrived(e_z, e1)
        for h in range(2):
            for i in range(4):
                send_or_copy(e_z.at[i, :, e_cols(h)], e_all.at[e_x[i], y0 * 2 + k, :, e_cols(h)], e_to[i], e2 + h)

    def e_enter(h):
        arrived(e_all.at[x, :, :, e_cols(h)], e2 + h)
        e_ring[h].start()

    s_ring = Gather(lambda i: s_all.at[:, i], lambda i: s_all.at[0, i], lambda i: s_all.at[1, i], x, x_up, x_down)
    a_ring = [
        Gather(
            lambda i, c=c: a_all.at[:, i, :, c], lambda i, c=c: a_all.at[0, i, :, c],
            lambda i, c=c: a_all.at[1, i, :, c], x, x_up, x_down,
        )
        for c in (a_cols(zh), a_cols(1 - zh))
    ]
    e_ring = [
        Gather(
            lambda i, h=h: e_all.at[i, :, :, e_cols(h)], lambda i, h=h: e_all.at[i, 0:2, :, e_cols(h)],
            lambda i, h=h: e_all.at[i, 2:4, :, e_cols(h)], x, x_up, x_down,
        )
        for h in range(2)
    ]

    def c_block(kk, j, i, part=slice(None), toks=slice(None)):
        return c_all.at[kk, i, part, toks, j * WIDE:(j + 1) * WIDE]

    c_ring = [
        Gather(
            lambda i, j=j: c_block(k, j, i), lambda i, j=j: c_block(k, j, i, slice(0, 2)),
            lambda i, j=j: c_block(k, j, i, slice(2, 4)), y, y_up, y_down,
        )
        for j in range(PARTS)
    ]
    t_ring = [
        Gather(
            lambda i, c=c: t_all.at[i, c * 256:c * 256 + 256], lambda i, c=c: t_all.at[i, c * 256:c * 256 + 128],
            lambda i, c=c: t_all.at[i, c * 256 + 128:c * 256 + 256], y, y_up, y_down,
        )
        for c in range(2)
    ]

    def u_cols(kk, i):
        return pl.ds(pl.multiple_of(kk * 512 + i * 128, 128), 128)

    def u_block(c, kk, i, tok=slice(None)):
        return u_all.at[tok, c * 256:c * 256 + 256, u_cols(kk, i)]

    u_ring = [
        Gather(
            lambda i, c=c: u_block(c, k, i), lambda i, c=c: u_block(c, k, i, 0), lambda i, c=c: u_block(c, k, i, 1),
            y, y_up, y_down,
        )
        for c in range(2)
    ]
    t_sum = Scatter(
        lambda i: t_part.at[i], lambda i: t_part.at[i, 0], lambda i: t_part.at[i, 1], t_tmp, t_two, y, y_up, y_down
    )
    g_sum = [
        Scatter(
            lambda i, j=j: g_part.at[j, i], lambda i, j=j: g_part.at[j, i, 0:WIDE],
            lambda i, j=j: g_part.at[j, i, WIDE:2 * WIDE], g_tmp.at[j], g_two.at[j], z, z_up, z_down,
        )
        for j in range(PARTS)
    ]
    o_sum = [
        Scatter(
            lambda i, c=c: o_part.at[c, i], lambda i, c=c: o_part.at[c, i, 0:128],
            lambda i, c=c: o_part.at[c, i, 128:256], o_tmp.at[c], o_two.at[c], z, z_up, z_down,
        )
        for c in range(2)
    ]

    def t_dots(d, kk, dst):
        for half in range(2):
            dst[d, half] = dot(act[...].reshape(512, 512), ei[d, half * 2 + kk], ((1,), (0,))).astype(dst.dtype)

    def t_join(d):
        arrived(t_sib_in.at[d], t1 + d)
        for half in range(2):
            t_part[ring(y, d), half] = (t_own[d, half] + t_sib_in[d, half].astype(F32)).astype(BF16)

    def ei_wait(d):
        for copy in ei_copies(d):
            copy.wait()

    act_copy.wait()
    ei_wait(2)
    t_dots(2, 1 - k, t_sib)
    t_dots(2, k, t_own)
    a_own_copy.wait()
    pl.semaphore_wait(barrier, expected)
    send(t_sib.at[2], t_sib_in.at[2], sib, t1 + 2)
    spread_send()
    c1_send(0)
    c2_send(0, 0)
    a_ring[0].start()
    for d in order[1:]:
        ei_wait(d)
        t_dots(d, 1 - k, t_sib)
        send(t_sib.at[d], t_sib_in.at[d], sib, t1 + d)
    t_join(2)
    t_sum.start()
    for d in order[1:]:
        t_dots(d, k, t_own)
    for d in order[1:]:
        t_join(d)
    arrived(c_spread, sp)
    c1_send(1)
    a1_send()
    c2_send(0, 1)
    arrived(c1_in.at[0], c1)
    c2_send(1, 0)
    t_sum.pass_up()
    t_sum.pass_down()
    arrived(c1_in.at[1], c1 + 1)
    c2_send(1, 1)
    e1_send()
    s1_send()

    def c_enter(j):
        if j == 0:
            arrived(c_all.at[k, y], c2)
        c_ring[j].start()
        send(c_block(k, j, y), c_block(k, j, y), sib, c4 + j)

    def c_pass(j):
        c_ring[j].pass_up()
        c_ring[j].pass_down()
        for d in (3, 1):
            send(c_block(k, j, ring(y, d)), c_block(k, j, ring(y, d)), sib, c4 + j)

    def c_finish(j):
        c_ring[j].finish()
        for half in (slice(0, 2), slice(2, 4)):
            send(c_block(k, j, ring(y, 2), half), c_block(k, j, ring(y, 2), half), sib, c4 + j)

    def c_sibling(j):
        arrived(c_all.at[1 - k, :, :, :, j * WIDE:(j + 1) * WIDE], c4 + j)

    def t_enter(c):
        rows = slice(c * 256, c * 256 + 256)
        arrived(t_swap_in.at[rows], t3 + c)
        t_all[y, rows] = (t_own[0, zh, rows] + t_swap_in[rows].astype(F32)).astype(BF16)
        t_ring[c].start()

    def g_block(j):
        parts = (
            (0, slice(None), a_all.at[0]),
            (1, slice(0, 64), a_all.at[1, :, 0:64]),
            (3, slice(64, 128), a_all.at[1, :, 64:128]),
        )
        for half in range(2):
            total = None
            for d, toks, acts in parts:
                block = jnp.concatenate(
                    [
                        c_block(kk, j, ring(2 * v + x1, d), toks=toks)[...].reshape(-1, WIDE)
                        for v in range(2)
                        for kk in range(2)
                    ],
                    axis=1,
                )
                part = dot(block, acts[:, :, half * 512:half * 512 + 512].reshape(-1, 512), ((0,), (0,)))
                total = part if total is None else total + part
            total = total.astype(BF16)
            for v in range(2):
                g_part[j, half * 2 + v] = total[v * 2 * WIDE:(v + 1) * 2 * WIDE]

    def g_enter(j):
        c_sibling(j)
        g_block(j)
        g_sum[j].start()

    def g_pass(j):
        g_sum[j].pass_up()
        g_sum[j].pass_down()

    def t_leave():
        t_sum.finish()
        for c in range(2):
            rows = slice(c * 256, c * 256 + 256)
            for half in range(2):
                t_own[0, half, rows] = (
                    t_part[y, half, rows].astype(F32)
                    + t_two[0, half, rows].astype(F32)
                    + t_two[1, half, rows].astype(F32)
                )
            t_swap[rows] = t_own[0, 1 - zh, rows].astype(BF16)
            send(t_swap.at[rows], t_swap_in.at[rows], z_far, t3 + c)

    def t_pass():
        for c in range(2):
            t_ring[c].pass_up()
            t_ring[c].pass_down()

    def both(gather):
        gather.pass_up()
        gather.pass_down()

    arrived(a_all.at[:, x, :, a_cols(1 - zh)], a1)
    a_ring[1].start()
    both(a_ring[0])
    c_enter(0)
    both(a_ring[1])
    t_leave()
    c_pass(0)
    c_enter(1)
    c_enter(2)
    arrived(s_all.at[:, x], s1)
    s_ring.start()
    c_finish(0)
    for ring_of_a in a_ring:
        ring_of_a.finish()
    g_enter(0)
    c_pass(1)
    t_enter(0)
    t_enter(1)
    c_pass(2)
    c_finish(1)
    g_pass(0)
    g_enter(1)
    t_pass()
    both(s_ring)
    e2_send()
    c_enter(3)
    c_finish(2)
    g_enter(2)
    g_pass(1)

    def u_dot(c, n):
        total = None
        for i in range(4):
            part = dot(
                t_all[i, c * 256:c * 256 + 256], s_all[n // 4, n % 4, :, i * 256:(i + 1) * 256], ((1,), (1,))
            )
            total = part if total is None else total + part
        return total

    for c in range(2):
        t_ring[c].finish()
        if c == 0:
            s_ring.finish()
        for n in range(8):
            u_own[c, n % 2, n // 2] = u_dot(c, n)
        u_sib[c] = u_own[c, 1 - k].astype(BF16)
        send(u_sib.at[c], u_sib_in.at[c], sib, u1 + c)
    e_enter(0)
    c_pass(3)
    for c in range(2):
        arrived(u_sib_in.at[c], u1 + c)
        u_part[c] = (u_own[c, k] + u_sib_in[c].astype(F32)).astype(BF16)
        for d in (1, 3, 2):
            send(u_part.at[c, ring(z, d)], u_in.at[c, d], at(z=ring(z, d)), u2 + c)
    g_pass(2)
    e_enter(1)
    c_finish(3)
    g_enter(3)

    def u_enter(c):
        rows = slice(c * 256, c * 256 + 256)
        arrived(u_in.at[c, 1:4], u2 + c)
        u_all[zl, rows, u_cols(k, y)] = (u_part[c, z].astype(F32) + u_in[c, 2].astype(F32)).astype(BF16)
        u_all[1 - zl, rows, u_cols(k, y)] = (u_in[c, 1].astype(F32) + u_in[c, 3].astype(F32)).astype(BF16)
        u_ring[c].start()
        send(u_block(c, k, y), u_block(c, k, y), sib, u4 + c)

    def u_pass(c):
        u_ring[c].pass_up()
        u_ring[c].pass_down()
        for d in (3, 1):
            send(u_block(c, k, ring(y, d)), u_block(c, k, ring(y, d)), sib, u4 + c)

    def u_finish(c):
        u_ring[c].finish()
        for n in range(2):
            half = u_block(c, k, ring(y, 2), n)
            send(half, half, sib, u4 + c)
        arrived(u_all.at[:, c * 256:c * 256 + 256, pl.ds(pl.multiple_of((1 - k) * 512, 512), 512)], u4 + c)

    u_enter(0)
    both(e_ring[0])
    u_enter(1)
    u_pass(0)
    both(e_ring[1])
    u_pass(1)
    g_pass(3)
    u_finish(0)
    for ring_of_e in e_ring:
        ring_of_e.finish()

    def o_block(c):
        for v in range(2):
            for w in range(2):
                slot = 2 * y0 + v
                if w:
                    slot = outer(slot)
                weight = e_all[slot].reshape(256, 1024)
                for tok in range(2):
                    total = dot(u_all[tok, c * 256:c * 256 + 256], weight, ((1,), (1,))).astype(BF16)
                    for n in range(2):
                        o_part[c, v * 2 + tok, :, n * 256 + w * 128:n * 256 + w * 128 + 128] = total[
                            :, n * 128:n * 128 + 128
                        ]

    o_block(0)
    o_sum[0].start()
    u_finish(1)
    o_block(1)
    o_sum[1].start()
    o_sum[0].pass_up()
    o_sum[0].pass_down()
    o_sum[1].pass_up()
    o_sum[1].pass_down()

    def last(dst, part, two, rows, first, to):
        @pl.loop(0, rows // 64)
        def _(i):
            src = pl.ds(pl.multiple_of(first + i * 64, 64), 64)
            dst[pl.ds(pl.multiple_of(to + i * 64, 64), 64)] = (
                part[src].astype(F32) + two[0, src].astype(F32) + two[1, src].astype(F32)
            ).astype(BF16)

    for j in range(PARTS):
        g_sum[j].finish()
        for kk in range(2):
            last(grad_ref, g_part.at[j, z], g_two.at[j], WIDE, kk * WIDE, kk * 512 + j * WIDE)
    for c in range(2):
        o_sum[c].finish()
        rows = slice(c * 256, c * 256 + 256)
        last(out_ref, o_part.at[c, z], o_two.at[c], 256, 0, c * 256)
    assert len(lone) <= LONE and len(loads) <= N_SEND - LONE
    for copy, when in lone:
        pl.when(when)(copy.wait_send)
    for n, size in enumerate(loads):
        rows = ei_hbm.at[0:size // 8192]
        remote(rows, rows, sib, LONE + n, 0).wait_send()


def per_device(small_weight, expand_out, expand_in, activations, cotangent):
    hbm = pl.BlockSpec(memory_space=pl.ANY)
    vmem = pl.BlockSpec(memory_space=pltpu.VMEM)

    def buf(*shape, dtype=BF16):
        return pltpu.VMEM(shape, dtype)

    return pl.pallas_call(
        kernel,
        out_shape=(
            pltpu.VMEM((512, 512), BF16),
            pltpu.VMEM((1024, 512), BF16),
        ),
        in_specs=[hbm] * 5,
        out_specs=(vmem, vmem),
        scratch_shapes=[
            buf(4, 4, 512, 256),
            buf(2, 2, 128, 512),
            pltpu.SemaphoreType.DMA((18,)),
            buf(2, 4, 128, 1024),
            buf(4, 64, 1024),
            buf(4, 4, 64, 1024),
            buf(2, 4, 128, 1024),
            buf(2, 4, 4, 128, 512),
            buf(2, 128, 512),
            buf(2, 128, 512),
            buf(4, 2, 512, 256),
            buf(4, 2, 512, 256),
            buf(4, 2, 512, 256, dtype=F32),
            buf(4, 2, 512, 256),
            buf(2, 512, 256),
            buf(2, 2, 512, 256),
            buf(512, 256),
            buf(512, 256),
            buf(4, 512, 256),
            buf(2, 2, 4, 256, 128, dtype=F32),
            buf(2, 4, 256, 128),
            buf(2, 4, 256, 128),
            buf(2, 4, 256, 128),
            buf(2, 4, 256, 128),
            buf(2, 512, 1024),
            buf(2, 4, 256, 512),
            buf(2, 2, 128, 512),
            buf(2, 2, 256, 512),
            buf(PARTS, 4, 2 * WIDE, 512),
            buf(PARTS, 2, WIDE, 512),
            buf(PARTS, 2, 2 * WIDE, 512),
            pltpu.SemaphoreType.DMA((N_SEND,)),
            pltpu.SemaphoreType.DMA((N_RECV,)),
        ],
        compiler_params=pltpu.CompilerParams(
            collective_id=0, has_side_effects=True, vmem_limit_bytes=58 * 2**20
        ),
        cost_estimate=pl.CostEstimate(flops=9_700_000_000, bytes_accessed=8_000_000, transcendentals=0),
        name="grow",
    )(
        small_weight,
        expand_out,
        expand_in,
        activations.reshape(2, 2, 128, 512),
        cotangent.reshape(2, 2, 128, 512),
    )

def solution(mesh):
    in_specs = (
        P(("row", "col"), None),
        P(("row", "col"), None),
        P("col", None),
        P("row", "col"),
        P("row", "col"),
    )
    out_specs = (P("row", "col"), P("row", "col"))
    return jax.shard_map(per_device, mesh=mesh, in_specs=in_specs, out_specs=out_specs, check_vma=False)
```

```python
import math

import jax
import jax.numpy as jnp
from jax import lax
from jax.experimental import pallas as pl
from jax.experimental.pallas import tpu as pltpu
from jax.sharding import PartitionSpec as P

MESH = pl.DeviceIdType.MESH
F32 = jnp.float32
BF16 = jnp.bfloat16
N_RECV, N_SEND, LONE = 96, 18, 12
GROUP = 4 * 2**20
PARTS = 4
WIDE = 512 // PARTS


def dot(a, b, dims):
    return lax.dot_general(a, b, (dims, ((), ())), preferred_element_type=F32)


def kernel(
    sw, eo, ei_hbm, act_hbm, cot, out_ref, grad_ref,
    ei, act, in_sem, s_all, e_z, e_all,  a_all, c_all, c_spread, c1_in,
    t_sib, t_sib_in, t_own, t_part, t_tmp, t_two, t_swap, t_swap_in, t_all,
    u_own, u_sib, u_sib_in, u_part, u_in, u_all,
    o_part, o_tmp, o_two, g_part, g_tmp, g_two,
    ssem, rsem,
):
    row, col = lax.axis_index("row"), lax.axis_index("col")
    x, zl = row % 4, row // 4
    k, zh, y = col % 2, (col // 2) % 2, col // 4
    z = zh * 2 + zl
    y0, y1, x0, x1 = y % 2, y // 2, x % 2, x // 2

    def at(x=x, y=y, z=z, k=k):
        return ((z % 2) * 4 + x, (y * 2 + z // 2) * 2 + k)

    def ring(i, d):
        return (i + d) % 4

    def outer(i):
        return ring(i, 3 + 2 * (i % 2))

    sib = at(k=1 - k)
    x_up, x_down = at(x=ring(x, 1)), at(x=ring(x, 3))
    y_up, y_down = at(y=ring(y, 1)), at(y=ring(y, 3))
    z_up, z_down = at(z=ring(z, 1)), at(z=ring(z, 3))
    z_far = at(z=ring(z, 2))

    c_x = [[2 * y0 + zh, 2 * (1 - y0) + zh], [2 * y0 + 1 - zh, 2 * (1 - y0) + 1 - zh]]
    c_home = x1 == y0
    e_x = [x, x, outer(x), outer(x)]
    e_to = [at(x=e_x[i], y=(i % 2) * 2 + x1, k=y1) for i in range(4)]
    e_src_x = jnp.where(c_home, x, outer(x))

    order = (2, 1, 3, 0)
    act_copy = pltpu.make_async_copy(act_hbm, act, in_sem.at[16])
    act_copy.start()

    def ei_copies(d):
        return [
            pltpu.make_async_copy(
                ei_hbm.at[:, pl.ds(pl.multiple_of(q * 1024 + ring(y, d) * 256, 256), 256)], ei.at[d, q], in_sem.at[d * 4 + q]
            )
            for q in range(4)
        ]

    def a_cols(half):
        return pl.ds(pl.multiple_of(half * 512, 512), 512)

    a_own_copy = pltpu.make_async_copy(act_hbm.at[zh], a_all.at[:, x, :, a_cols(zh)], in_sem.at[17])
    a_own_copy.start()
    for d in order:
        for copy in ei_copies(d):
            copy.start()

    barrier = pltpu.get_barrier_semaphore()

    def greet(to):
        pl.semaphore_signal(barrier, inc=1, device_id=to, device_id_type=MESH)

    expected = 0
    for dz in range(4):
        for dk in range(2):
            if dz or dk:
                greet(at(z=ring(z, dz), k=(k + dk) % 2))
                expected += 1
    for to in (x_up, x_down, y_up, y_down):
        greet(to)
        expected += 1

    def greet_unless_self(to):
        other = jnp.logical_or(to[0] != row, to[1] != col)

        @pl.when(other)
        def _():
            greet(to)

        return other.astype(jnp.int32)

    for d in (2,):
        greet(at(x=ring(x, d)))
        expected += 1
    for to in e_to:
        expected += greet_unless_self(to)
    for i in range(4):
        expected += greet_unless_self(at(x=e_src_x, y=2 * k + i // 2, k=i % 2))
    count = [0]
    loads = [0]
    lone = []

    def ids(n):
        first = count[0]
        count[0] += n
        assert count[0] <= N_RECV
        return first

    def remote(src, dst, to, s, r):
        return pltpu.make_async_remote_copy(
            src_ref=src, dst_ref=dst, send_sem=ssem.at[s], recv_sem=rsem.at[r],
            device_id=to, device_id_type=MESH,
        )

    def send(src, dst, to, r):
        size = 2 * math.prod(src.shape)
        if loads[-1] + size > GROUP:
            loads.append(0)
        loads[-1] += size
        remote(src, dst, to, LONE + len(loads) - 1, r).start()

    def send_or_copy(src, dst, to, r):
        mine = jnp.logical_and(to[0] == row, to[1] == col)
        copy = remote(src, dst, to, len(lone), r)

        @pl.when(mine)
        def _():
            pltpu.make_async_copy(src, dst, rsem.at[r]).start()

        @pl.when(jnp.logical_not(mine))
        def _():
            copy.start()

        lone.append((copy, jnp.logical_not(mine)))

    def arrived(ref, r):
        remote(ref, ref, sib, 0, r).wait_recv()

    class Gather:
        def __init__(self, slot, first, second, me, up, down):
            self.slot, self.first, self.second, self.me = slot, first, second, me
            self.up, self.down, self.s = up, down, ids(3)

        def start(self):
            mine = self.slot(self.me)
            send(mine, mine, self.up, self.s)
            send(mine, mine, self.down, self.s + 1)

        def pass_up(self):
            i = ring(self.me, 3)
            arrived(self.slot(i), self.s)
            send(self.first(i), self.first(i), self.up, self.s + 2)

        def pass_down(self):
            i = ring(self.me, 1)
            arrived(self.slot(i), self.s + 1)
            send(self.second(i), self.second(i), self.down, self.s + 2)

        def finish(self):
            arrived(self.slot(ring(self.me, 2)), self.s + 2)

    class Scatter:
        def __init__(self, slot, first, second, tmp, two, me, up, down):
            self.slot, self.first, self.second = slot, first, second
            self.tmp, self.two, self.me, self.up, self.down, self.s = tmp, two, me, up, down, ids(3)

        def start(self):
            i = ring(self.me, 2)
            send(self.first(i), self.tmp.at[0], self.up, self.s)
            send(self.second(i), self.tmp.at[1], self.down, self.s + 1)

        def pass_up(self):
            i = ring(self.me, 1)
            arrived(self.tmp.at[0], self.s)
            add_into(self.first(i), self.tmp.at[0])
            send(self.slot(i), self.two.at[0], self.up, self.s + 2)

        def pass_down(self):
            i = ring(self.me, 3)
            arrived(self.tmp.at[1], self.s + 1)
            add_into(self.second(i), self.tmp.at[1])
            send(self.slot(i), self.two.at[1], self.down, self.s + 2)

        def finish(self):
            arrived(self.two, self.s + 2)

    def add_into(dst, src):
        rows = dst.shape[0]

        @pl.loop(0, rows // 64)
        def _(i):
            part = pl.ds(pl.multiple_of(i * 64, 64), 64)
            dst[part] = (dst[part].astype(F32) + src[part].astype(F32)).astype(BF16)

    sp, c1, a1, s1, e1, e2, c2 = ids(1), ids(2), ids(1), ids(1), ids(1), ids(2), ids(1)
    t1, t3, u1 = ids(4), ids(2), ids(2)
    u2, u4 = ids(2), ids(2)
    c4 = ids(PARTS)
    s_home = s_all.at[zl, x, pl.ds(pl.multiple_of(zh * 64 + k * 32, 32), 32)]

    def spread_send():
        for n, to in enumerate((y_up, y_down)):
            send(cot.at[:, 1, n * 64:n * 64 + 64], c_spread.at[:, n * 64:n * 64 + 64], to, sp)

    def c1_send(half):
        src = cot.at[1 - zh, 0] if half == 0 else c_spread.at[1 - zh]
        send(src, c1_in.at[half], z_far, c1 + half)

    def a1_send():
        send(act_hbm.at[1 - zh], a_all.at[:, x, :, a_cols(zh)], z_far, a1)

    def c2_send(other, half):
        if other:
            src = c1_in.at[half]
        else:
            src = c_spread.at[zh] if half else cot.at[zh, 0]
        send_or_copy(src, c_all.at[k, y, x], at(x=c_x[other][half]), c2)

    def s1_send():
        for dz in (1, 3, 2, 0):
            for dk in range(2):
                tz, tk = ring(z, dz), (k + dk) % 2
                piece = sw.at[:, pl.ds(pl.multiple_of(((tz // 2) * 2 + tk) * 1024, 1024), 1024)]
                if dz or dk:
                    send(piece, s_home, at(z=tz, k=tk), s1)
                else:
                    pltpu.make_async_copy(piece, s_home, rsem.at[s1]).start()

    def e1_send():
        for d in (1, 3, 2, 0):
            i = ring(z, d)
            piece = eo.at[:, pl.ds(pl.multiple_of(i * 1024, 1024), 1024)]
            if d:
                send(piece, e_z.at[z], at(z=i), e1)
            else:
                pltpu.make_async_copy(piece, e_z.at[z], rsem.at[e1]).start()

    def e_cols(h):
        return slice(h * 512, h * 512 + 512)

    def e2_send():
        arrived(e_z, e1)
        for h in range(2):
            for i in range(4):
                send_or_copy(e_z.at[i, :, e_cols(h)], e_all.at[e_x[i], y0 * 2 + k, :, e_cols(h)], e_to[i], e2 + h)

    def e_enter(h):
        arrived(e_all.at[x, :, :, e_cols(h)], e2 + h)
        e_ring[h].start()

    s_ring = Gather(lambda i: s_all.at[:, i], lambda i: s_all.at[0, i], lambda i: s_all.at[1, i], x, x_up, x_down)
    a_ring = [
        Gather(
            lambda i, c=c: a_all.at[:, i, :, c], lambda i, c=c: a_all.at[0, i, :, c],
            lambda i, c=c: a_all.at[1, i, :, c], x, x_up, x_down,
        )
        for c in (a_cols(zh), a_cols(1 - zh))
    ]
    e_ring = [
        Gather(
            lambda i, h=h: e_all.at[i, :, :, e_cols(h)], lambda i, h=h: e_all.at[i, 0:2, :, e_cols(h)],
            lambda i, h=h: e_all.at[i, 2:4, :, e_cols(h)], x, x_up, x_down,
        )
        for h in range(2)
    ]

    def c_block(kk, j, i, part=slice(None), toks=slice(None)):
        return c_all.at[kk, i, part, toks, j * WIDE:(j + 1) * WIDE]

    c_ring = [
        Gather(
            lambda i, j=j: c_block(k, j, i), lambda i, j=j: c_block(k, j, i, slice(0, 2)),
            lambda i, j=j: c_block(k, j, i, slice(2, 4)), y, y_up, y_down,
        )
        for j in range(PARTS)
    ]
    t_ring = [
        Gather(
            lambda i, c=c: t_all.at[i, c * 256:c * 256 + 256], lambda i, c=c: t_all.at[i, c * 256:c * 256 + 128],
            lambda i, c=c: t_all.at[i, c * 256 + 128:c * 256 + 256], y, y_up, y_down,
        )
        for c in range(2)
    ]

    def u_cols(kk, i):
        return pl.ds(pl.multiple_of(kk * 512 + i * 128, 128), 128)

    def u_block(c, kk, i, tok=slice(None)):
        return u_all.at[tok, c * 256:c * 256 + 256, u_cols(kk, i)]

    u_ring = [
        Gather(
            lambda i, c=c: u_block(c, k, i), lambda i, c=c: u_block(c, k, i, 0), lambda i, c=c: u_block(c, k, i, 1),
            y, y_up, y_down,
        )
        for c in range(2)
    ]
    t_sum = Scatter(
        lambda i: t_part.at[i], lambda i: t_part.at[i, 0], lambda i: t_part.at[i, 1], t_tmp, t_two, y, y_up, y_down
    )
    g_sum = [
        Scatter(
            lambda i, j=j: g_part.at[j, i], lambda i, j=j: g_part.at[j, i, 0:WIDE],
            lambda i, j=j: g_part.at[j, i, WIDE:2 * WIDE], g_tmp.at[j], g_two.at[j], z, z_up, z_down,
        )
        for j in range(PARTS)
    ]
    o_sum = [
        Scatter(
            lambda i, c=c: o_part.at[c, i], lambda i, c=c: o_part.at[c, i, 0:128],
            lambda i, c=c: o_part.at[c, i, 128:256], o_tmp.at[c], o_two.at[c], z, z_up, z_down,
        )
        for c in range(2)
    ]

    def t_dots(d, kk, dst):
        for half in range(2):
            dst[d, half] = dot(act[...].reshape(512, 512), ei[d, half * 2 + kk], ((1,), (0,))).astype(dst.dtype)

    def t_join(d):
        arrived(t_sib_in.at[d], t1 + d)
        for half in range(2):
            t_part[ring(y, d), half] = (t_own[d, half] + t_sib_in[d, half].astype(F32)).astype(BF16)

    def ei_wait(d):
        for copy in ei_copies(d):
            copy.wait()

    act_copy.wait()
    ei_wait(2)
    t_dots(2, 1 - k, t_sib)
    t_dots(2, k, t_own)
    a_own_copy.wait()
    pl.semaphore_wait(barrier, expected)
    send(t_sib.at[2], t_sib_in.at[2], sib, t1 + 2)
    c1_send(0)
    spread_send()
    c2_send(0, 0)
    a_ring[0].start()
    for d in order[1:]:
        ei_wait(d)
        t_dots(d, 1 - k, t_sib)
        send(t_sib.at[d], t_sib_in.at[d], sib, t1 + d)
    t_join(2)
    t_sum.start()
    for d in order[1:]:
        t_dots(d, k, t_own)
    for d in order[1:]:
        t_join(d)
    arrived(c_spread, sp)
    c1_send(1)
    a1_send()
    c2_send(0, 1)
    arrived(c1_in.at[0], c1)
    c2_send(1, 0)
    t_sum.pass_up()
    t_sum.pass_down()
    arrived(c1_in.at[1], c1 + 1)
    c2_send(1, 1)
    e1_send()
    s1_send()

    def c_enter(j):
        if j == 0:
            arrived(c_all.at[k, y], c2)
        c_ring[j].start()
        send(c_block(k, j, y), c_block(k, j, y), sib, c4 + j)

    def c_pass(j):
        c_ring[j].pass_up()
        c_ring[j].pass_down()
        for d in (3, 1):
            send(c_block(k, j, ring(y, d)), c_block(k, j, ring(y, d)), sib, c4 + j)

    def c_finish(j):
        c_ring[j].finish()
        for half in (slice(0, 2), slice(2, 4)):
            send(c_block(k, j, ring(y, 2), half), c_block(k, j, ring(y, 2), half), sib, c4 + j)

    def c_sibling(j):
        arrived(c_all.at[1 - k, :, :, :, j * WIDE:(j + 1) * WIDE], c4 + j)

    def t_enter(c):
        rows = slice(c * 256, c * 256 + 256)
        arrived(t_swap_in.at[rows], t3 + c)
        t_all[y, rows] = (t_own[0, zh, rows] + t_swap_in[rows].astype(F32)).astype(BF16)
        t_ring[c].start()

    def g_block(j):
        parts = (
            (0, slice(None), a_all.at[0]),
            (1, slice(0, 64), a_all.at[1, :, 0:64]),
            (3, slice(64, 128), a_all.at[1, :, 64:128]),
        )
        for half in range(2):
            total = None
            for d, toks, acts in parts:
                block = jnp.concatenate(
                    [
                        c_block(kk, j, ring(2 * v + x1, d), toks=toks)[...].reshape(-1, WIDE)
                        for v in range(2)
                        for kk in range(2)
                    ],
                    axis=1,
                )
                part = dot(block, acts[:, :, half * 512:half * 512 + 512].reshape(-1, 512), ((0,), (0,)))
                total = part if total is None else total + part
            total = total.astype(BF16)
            for v in range(2):
                g_part[j, half * 2 + v] = total[v * 2 * WIDE:(v + 1) * 2 * WIDE]

    def g_enter(j):
        c_sibling(j)
        g_block(j)
        g_sum[j].start()

    def g_pass(j):
        g_sum[j].pass_up()
        g_sum[j].pass_down()

    def t_leave():
        t_sum.finish()
        for c in range(2):
            rows = slice(c * 256, c * 256 + 256)
            for half in range(2):
                t_own[0, half, rows] = (
                    t_part[y, half, rows].astype(F32)
                    + t_two[0, half, rows].astype(F32)
                    + t_two[1, half, rows].astype(F32)
                )
            t_swap[rows] = t_own[0, 1 - zh, rows].astype(BF16)
            send(t_swap.at[rows], t_swap_in.at[rows], z_far, t3 + c)

    def t_pass():
        for c in range(2):
            t_ring[c].pass_up()
            t_ring[c].pass_down()

    def both(gather):
        gather.pass_up()
        gather.pass_down()

    arrived(a_all.at[:, x, :, a_cols(1 - zh)], a1)
    a_ring[1].start()
    both(a_ring[0])
    c_enter(0)
    both(a_ring[1])
    t_leave()
    c_pass(0)
    c_enter(1)
    c_enter(2)
    arrived(s_all.at[:, x], s1)
    s_ring.start()
    c_finish(0)
    for ring_of_a in a_ring:
        ring_of_a.finish()
    g_enter(0)
    c_pass(1)
    t_enter(0)
    t_enter(1)
    c_pass(2)
    c_finish(1)
    g_pass(0)
    g_enter(1)
    t_pass()
    both(s_ring)
    e2_send()
    c_enter(3)
    c_finish(2)
    g_enter(2)
    g_pass(1)

    def u_dot(c, n):
        total = None
        for i in range(4):
            part = dot(
                t_all[i, c * 256:c * 256 + 256], s_all[n // 4, n % 4, :, i * 256:(i + 1) * 256], ((1,), (1,))
            )
            total = part if total is None else total + part
        return total

    for c in range(2):
        t_ring[c].finish()
        if c == 0:
            s_ring.finish()
        for n in range(8):
            u_own[c, n % 2, n // 2] = u_dot(c, n)
        u_sib[c] = u_own[c, 1 - k].astype(BF16)
        send(u_sib.at[c], u_sib_in.at[c], sib, u1 + c)
    e_enter(0)
    c_pass(3)
    for c in range(2):
        arrived(u_sib_in.at[c], u1 + c)
        u_part[c] = (u_own[c, k] + u_sib_in[c].astype(F32)).astype(BF16)
        for d in (2, 1, 3):
            send(u_part.at[c, ring(z, d)], u_in.at[c, d], at(z=ring(z, d)), u2 + c)
    g_pass(2)
    e_enter(1)
    c_finish(3)
    g_enter(3)

    def u_enter(c):
        rows = slice(c * 256, c * 256 + 256)
        arrived(u_in.at[c, 1:4], u2 + c)
        u_all[zl, rows, u_cols(k, y)] = (u_part[c, z].astype(F32) + u_in[c, 2].astype(F32)).astype(BF16)
        u_all[1 - zl, rows, u_cols(k, y)] = (u_in[c, 1].astype(F32) + u_in[c, 3].astype(F32)).astype(BF16)
        u_ring[c].start()
        send(u_block(c, k, y), u_block(c, k, y), sib, u4 + c)

    def u_pass(c):
        u_ring[c].pass_up()
        u_ring[c].pass_down()
        for d in (3, 1):
            send(u_block(c, k, ring(y, d)), u_block(c, k, ring(y, d)), sib, u4 + c)

    def u_finish(c):
        u_ring[c].finish()
        for n in range(2):
            half = u_block(c, k, ring(y, 2), n)
            send(half, half, sib, u4 + c)
        arrived(u_all.at[:, c * 256:c * 256 + 256, pl.ds(pl.multiple_of((1 - k) * 512, 512), 512)], u4 + c)

    u_enter(0)
    both(e_ring[0])
    u_enter(1)
    u_pass(0)
    both(e_ring[1])
    u_pass(1)
    g_pass(3)
    u_finish(0)
    for ring_of_e in e_ring:
        ring_of_e.finish()

    def o_shard(c, v, tok):
        for w in range(2):
            slot = 2 * y0 + v
            if w:
                slot = outer(slot)
            weight = e_all[slot].reshape(256, 1024)
            total = dot(u_all[tok, c * 256:c * 256 + 256], weight, ((1,), (1,))).astype(BF16)
            for n in range(2):
                o_part[c, v * 2 + tok, :, n * 256 + w * 128:n * 256 + w * 128 + 128] = total[:, n * 128:n * 128 + 128]

    def o_enter(c):
        o_shard(c, 1 - zh, zl)
        o_sum[c].start()
        for v, tok in ((zh, 1 - zl), (1 - zh, 1 - zl), (zh, zl)):
            o_shard(c, v, tok)

    o_enter(0)
    u_finish(1)
    o_enter(1)
    o_sum[0].pass_up()
    o_sum[0].pass_down()
    o_sum[1].pass_up()
    o_sum[1].pass_down()

    def last(dst, part, two, rows, first, to):
        @pl.loop(0, rows // 64)
        def _(i):
            src = pl.ds(pl.multiple_of(first + i * 64, 64), 64)
            dst[pl.ds(pl.multiple_of(to + i * 64, 64), 64)] = (
                part[src].astype(F32) + two[0, src].astype(F32) + two[1, src].astype(F32)
            ).astype(BF16)

    for j in range(PARTS):
        g_sum[j].finish()
        for kk in range(2):
            last(grad_ref, g_part.at[j, z], g_two.at[j], WIDE, kk * WIDE, kk * 512 + j * WIDE)
    for c in range(2):
        o_sum[c].finish()
        rows = slice(c * 256, c * 256 + 256)
        last(out_ref, o_part.at[c, z], o_two.at[c], 256, 0, c * 256)
    assert len(lone) <= LONE and len(loads) <= N_SEND - LONE
    for copy, when in lone:
        pl.when(when)(copy.wait_send)
    for n, size in enumerate(loads):
        rows = ei_hbm.at[0:size // 8192]
        remote(rows, rows, sib, LONE + n, 0).wait_send()


def per_device(small_weight, expand_out, expand_in, activations, cotangent):
    hbm = pl.BlockSpec(memory_space=pl.ANY)
    vmem = pl.BlockSpec(memory_space=pltpu.VMEM)

    def buf(*shape, dtype=BF16):
        return pltpu.VMEM(shape, dtype)

    return pl.pallas_call(
        kernel,
        out_shape=(
            pltpu.VMEM((512, 512), BF16),
            pltpu.VMEM((1024, 512), BF16),
        ),
        in_specs=[hbm] * 5,
        out_specs=(vmem, vmem),
        scratch_shapes=[
            buf(4, 4, 512, 256),
            buf(2, 2, 128, 512),
            pltpu.SemaphoreType.DMA((18,)),
            buf(2, 4, 128, 1024),
            buf(4, 64, 1024),
            buf(4, 4, 64, 1024),
            buf(2, 4, 128, 1024),
            buf(2, 4, 4, 128, 512),
            buf(2, 128, 512),
            buf(2, 128, 512),
            buf(4, 2, 512, 256),
            buf(4, 2, 512, 256),
            buf(4, 2, 512, 256, dtype=F32),
            buf(4, 2, 512, 256),
            buf(2, 512, 256),
            buf(2, 2, 512, 256),
            buf(512, 256),
            buf(512, 256),
            buf(4, 512, 256),
            buf(2, 2, 4, 256, 128, dtype=F32),
            buf(2, 4, 256, 128),
            buf(2, 4, 256, 128),
            buf(2, 4, 256, 128),
            buf(2, 4, 256, 128),
            buf(2, 512, 1024),
            buf(2, 4, 256, 512),
            buf(2, 2, 128, 512),
            buf(2, 2, 256, 512),
            buf(PARTS, 4, 2 * WIDE, 512),
            buf(PARTS, 2, WIDE, 512),
            buf(PARTS, 2, 2 * WIDE, 512),
            pltpu.SemaphoreType.DMA((N_SEND,)),
            pltpu.SemaphoreType.DMA((N_RECV,)),
        ],
        compiler_params=pltpu.CompilerParams(
            collective_id=0, has_side_effects=True, vmem_limit_bytes=58 * 2**20
        ),
        cost_estimate=pl.CostEstimate(flops=9_700_000_000, bytes_accessed=8_000_000, transcendentals=0),
        name="grow",
    )(
        small_weight,
        expand_out,
        expand_in,
        activations.reshape(2, 2, 128, 512),
        cotangent.reshape(2, 2, 128, 512),
    )

def solution(mesh):
    in_specs = (
        P(("row", "col"), None),
        P(("row", "col"), None),
        P("col", None),
        P("row", "col"),
        P("row", "col"),
    )
    out_specs = (P("row", "col"), P("row", "col"))
    return jax.shard_map(per_device, mesh=mesh, in_specs=in_specs, out_specs=out_specs, check_vma=False)
```

```python
import math

import jax
import jax.numpy as jnp
from jax import lax
from jax.experimental import pallas as pl
from jax.experimental.pallas import tpu as pltpu
from jax.sharding import PartitionSpec as P

MESH = pl.DeviceIdType.MESH
F32 = jnp.float32
BF16 = jnp.bfloat16
N_RECV, N_SEND, LONE = 96, 18, 12
GROUP = 4 * 2**20
PARTS = 4
WIDE = 512 // PARTS


def dot(a, b, dims):
    return lax.dot_general(a, b, (dims, ((), ())), preferred_element_type=F32)


def kernel(
    sw, eo, ei_hbm, act_hbm, cot, out_ref, grad_ref,
    ei, act, in_sem, s_all, e_z, e_all,  a_all, c_all, c_spread, c1_in,
    t_sib, t_sib_in, t_own, t_part, t_tmp, t_two, t_swap, t_swap_in, t_all,
    u_own, u_sib, u_sib_in, u_part, u_in, u_all,
    o_part, o_tmp, o_two, g_part, g_tmp, g_two,
    ssem, rsem,
):
    row, col = lax.axis_index("row"), lax.axis_index("col")
    x, zl = row % 4, row // 4
    k, zh, y = col % 2, (col // 2) % 2, col // 4
    z = zh * 2 + zl
    y0, y1, x0, x1 = y % 2, y // 2, x % 2, x // 2

    def at(x=x, y=y, z=z, k=k):
        return ((z % 2) * 4 + x, (y * 2 + z // 2) * 2 + k)

    def ring(i, d):
        return (i + d) % 4

    def outer(i):
        return ring(i, 3 + 2 * (i % 2))

    sib = at(k=1 - k)
    x_up, x_down = at(x=ring(x, 1)), at(x=ring(x, 3))
    y_up, y_down = at(y=ring(y, 1)), at(y=ring(y, 3))
    z_up, z_down = at(z=ring(z, 1)), at(z=ring(z, 3))
    z_far = at(z=ring(z, 2))

    c_x = [[2 * y0 + zh, 2 * (1 - y0) + zh], [2 * y0 + 1 - zh, 2 * (1 - y0) + 1 - zh]]
    c_home = x1 == y0
    e_x = [x, x, outer(x), outer(x)]
    e_to = [at(x=e_x[i], y=(i % 2) * 2 + x1, k=y1) for i in range(4)]
    e_src_x = jnp.where(c_home, x, outer(x))

    order = (2, 1, 3, 0)
    act_copy = pltpu.make_async_copy(act_hbm, act, in_sem.at[16])
    act_copy.start()

    def ei_copies(d):
        return [
            pltpu.make_async_copy(
                ei_hbm.at[:, pl.ds(pl.multiple_of(q * 1024 + ring(y, d) * 256, 256), 256)], ei.at[d, q], in_sem.at[d * 4 + q]
            )
            for q in range(4)
        ]

    def a_cols(half):
        return pl.ds(pl.multiple_of(half * 512, 512), 512)

    a_own_copy = pltpu.make_async_copy(act_hbm.at[zh], a_all.at[:, x, :, a_cols(zh)], in_sem.at[17])
    a_own_copy.start()
    for d in order:
        for copy in ei_copies(d):
            copy.start()

    barrier = pltpu.get_barrier_semaphore()

    def greet(to):
        pl.semaphore_signal(barrier, inc=1, device_id=to, device_id_type=MESH)

    expected = 0
    for dz in range(4):
        for dk in range(2):
            if dz or dk:
                greet(at(z=ring(z, dz), k=(k + dk) % 2))
                expected += 1
    for to in (x_up, x_down, y_up, y_down):
        greet(to)
        expected += 1

    def greet_unless_self(to):
        other = jnp.logical_or(to[0] != row, to[1] != col)

        @pl.when(other)
        def _():
            greet(to)

        return other.astype(jnp.int32)

    for d in (2,):
        greet(at(x=ring(x, d)))
        expected += 1
    for to in e_to:
        expected += greet_unless_self(to)
    for i in range(4):
        expected += greet_unless_self(at(x=e_src_x, y=2 * k + i // 2, k=i % 2))
    count = [0]
    loads = [0]
    lone = []

    def ids(n):
        first = count[0]
        count[0] += n
        assert count[0] <= N_RECV
        return first

    def remote(src, dst, to, s, r):
        return pltpu.make_async_remote_copy(
            src_ref=src, dst_ref=dst, send_sem=ssem.at[s], recv_sem=rsem.at[r],
            device_id=to, device_id_type=MESH,
        )

    def send(src, dst, to, r):
        size = 2 * math.prod(src.shape)
        if loads[-1] + size > GROUP:
            loads.append(0)
        loads[-1] += size
        remote(src, dst, to, LONE + len(loads) - 1, r).start()

    def send_or_copy(src, dst, to, r):
        mine = jnp.logical_and(to[0] == row, to[1] == col)
        copy = remote(src, dst, to, len(lone), r)

        @pl.when(mine)
        def _():
            pltpu.make_async_copy(src, dst, rsem.at[r]).start()

        @pl.when(jnp.logical_not(mine))
        def _():
            copy.start()

        lone.append((copy, jnp.logical_not(mine)))

    def arrived(ref, r):
        remote(ref, ref, sib, 0, r).wait_recv()

    class Gather:
        def __init__(self, slot, first, second, me, up, down):
            self.slot, self.first, self.second, self.me = slot, first, second, me
            self.up, self.down, self.s = up, down, ids(3)

        def start(self):
            mine = self.slot(self.me)
            send(mine, mine, self.up, self.s)
            send(mine, mine, self.down, self.s + 1)

        def pass_up(self):
            i = ring(self.me, 3)
            arrived(self.slot(i), self.s)
            send(self.first(i), self.first(i), self.up, self.s + 2)

        def pass_down(self):
            i = ring(self.me, 1)
            arrived(self.slot(i), self.s + 1)
            send(self.second(i), self.second(i), self.down, self.s + 2)

        def finish(self):
            arrived(self.slot(ring(self.me, 2)), self.s + 2)

    class Scatter:
        def __init__(self, slot, first, second, tmp, two, me, up, down):
            self.slot, self.first, self.second = slot, first, second
            self.tmp, self.two, self.me, self.up, self.down, self.s = tmp, two, me, up, down, ids(3)

        def start(self):
            i = ring(self.me, 2)
            send(self.first(i), self.tmp.at[0], self.up, self.s)
            send(self.second(i), self.tmp.at[1], self.down, self.s + 1)

        def pass_up(self):
            i = ring(self.me, 1)
            arrived(self.tmp.at[0], self.s)
            add_into(self.first(i), self.tmp.at[0])
            send(self.slot(i), self.two.at[0], self.up, self.s + 2)

        def pass_down(self):
            i = ring(self.me, 3)
            arrived(self.tmp.at[1], self.s + 1)
            add_into(self.second(i), self.tmp.at[1])
            send(self.slot(i), self.two.at[1], self.down, self.s + 2)

        def finish(self):
            arrived(self.two, self.s + 2)

    def add_into(dst, src):
        rows = dst.shape[0]

        @pl.loop(0, rows // 64)
        def _(i):
            part = pl.ds(pl.multiple_of(i * 64, 64), 64)
            dst[part] = (dst[part].astype(F32) + src[part].astype(F32)).astype(BF16)

    sp, c1, a1, s1, e1, e2, c2 = ids(1), ids(2), ids(1), ids(1), ids(1), ids(2), ids(1)
    t1, t3, u1 = ids(4), ids(2), ids(2)
    u2, u4 = ids(2), ids(2)
    c4 = ids(PARTS)
    s_home = s_all.at[zl, x, pl.ds(pl.multiple_of(zh * 64 + k * 32, 32), 32)]

    def spread_send():
        for n, to in enumerate((y_up, y_down)):
            send(cot.at[:, 1, n * 64:n * 64 + 64], c_spread.at[:, n * 64:n * 64 + 64], to, sp)

    def c1_send(half):
        src = cot.at[1 - zh, 0] if half == 0 else c_spread.at[1 - zh]
        send(src, c1_in.at[half], z_far, c1 + half)

    def a1_send():
        send(act_hbm.at[1 - zh], a_all.at[:, x, :, a_cols(zh)], z_far, a1)

    def c2_send(other, half):
        if other:
            src = c1_in.at[half]
        else:
            src = c_spread.at[zh] if half else cot.at[zh, 0]
        send_or_copy(src, c_all.at[k, y, x], at(x=c_x[other][half]), c2)

    def s1_send():
        for dz in (1, 3, 2, 0):
            for dk in range(2):
                tz, tk = ring(z, dz), (k + dk) % 2
                piece = sw.at[:, pl.ds(pl.multiple_of(((tz // 2) * 2 + tk) * 1024, 1024), 1024)]
                if dz or dk:
                    send(piece, s_home, at(z=tz, k=tk), s1)
                else:
                    pltpu.make_async_copy(piece, s_home, rsem.at[s1]).start()

    def e1_send():
        for d in (1, 3, 2, 0):
            i = ring(z, d)
            piece = eo.at[:, pl.ds(pl.multiple_of(i * 1024, 1024), 1024)]
            if d:
                send(piece, e_z.at[z], at(z=i), e1)
            else:
                pltpu.make_async_copy(piece, e_z.at[z], rsem.at[e1]).start()

    def e_cols(h):
        return slice(h * 512, h * 512 + 512)

    def e2_send():
        arrived(e_z, e1)
        for h in range(2):
            for i in range(4):
                send_or_copy(e_z.at[i, :, e_cols(h)], e_all.at[e_x[i], y0 * 2 + k, :, e_cols(h)], e_to[i], e2 + h)

    def e_enter(h):
        arrived(e_all.at[x, :, :, e_cols(h)], e2 + h)
        e_ring[h].start()

    s_ring = Gather(lambda i: s_all.at[:, i], lambda i: s_all.at[0, i], lambda i: s_all.at[1, i], x, x_up, x_down)
    a_ring = [
        Gather(
            lambda i, c=c: a_all.at[:, i, :, c], lambda i, c=c: a_all.at[0, i, :, c],
            lambda i, c=c: a_all.at[1, i, :, c], x, x_up, x_down,
        )
        for c in (a_cols(zh), a_cols(1 - zh))
    ]
    e_ring = [
        Gather(
            lambda i, h=h: e_all.at[i, :, :, e_cols(h)], lambda i, h=h: e_all.at[i, 0:2, :, e_cols(h)],
            lambda i, h=h: e_all.at[i, 2:4, :, e_cols(h)], x, x_up, x_down,
        )
        for h in range(2)
    ]

    def c_block(kk, j, i, part=slice(None), toks=slice(None)):
        return c_all.at[kk, i, part, toks, j * WIDE:(j + 1) * WIDE]

    c_ring = [
        Gather(
            lambda i, j=j: c_block(k, j, i), lambda i, j=j: c_block(k, j, i, slice(0, 2)),
            lambda i, j=j: c_block(k, j, i, slice(2, 4)), y, y_up, y_down,
        )
        for j in range(PARTS)
    ]
    t_ring = [
        Gather(
            lambda i, c=c: t_all.at[i, c * 256:c * 256 + 256], lambda i, c=c: t_all.at[i, c * 256:c * 256 + 128],
            lambda i, c=c: t_all.at[i, c * 256 + 128:c * 256 + 256], y, y_up, y_down,
        )
        for c in range(2)
    ]

    def u_cols(kk, i):
        return pl.ds(pl.multiple_of(kk * 512 + i * 128, 128), 128)

    def u_block(c, kk, i, tok=slice(None)):
        return u_all.at[tok, c * 256:c * 256 + 256, u_cols(kk, i)]

    u_ring = [
        Gather(
            lambda i, c=c: u_block(c, k, i), lambda i, c=c: u_block(c, k, i, 0), lambda i, c=c: u_block(c, k, i, 1),
            y, y_up, y_down,
        )
        for c in range(2)
    ]
    t_sum = Scatter(
        lambda i: t_part.at[i], lambda i: t_part.at[i, 0], lambda i: t_part.at[i, 1], t_tmp, t_two, y, y_up, y_down
    )
    g_sum = [
        Scatter(
            lambda i, j=j: g_part.at[j, i], lambda i, j=j: g_part.at[j, i, 0:WIDE],
            lambda i, j=j: g_part.at[j, i, WIDE:2 * WIDE], g_tmp.at[j], g_two.at[j], z, z_up, z_down,
        )
        for j in range(PARTS)
    ]
    o_sum = [
        Scatter(
            lambda i, c=c: o_part.at[c, i], lambda i, c=c: o_part.at[c, i, 0:128],
            lambda i, c=c: o_part.at[c, i, 128:256], o_tmp.at[c], o_two.at[c], z, z_up, z_down,
        )
        for c in range(2)
    ]

    def t_dots(d, kk, dst):
        for half in range(2):
            dst[d, half] = dot(act[...].reshape(512, 512), ei[d, half * 2 + kk], ((1,), (0,))).astype(dst.dtype)

    def t_join(d):
        arrived(t_sib_in.at[d], t1 + d)
        for half in range(2):
            t_part[ring(y, d), half] = (t_own[d, half] + t_sib_in[d, half].astype(F32)).astype(BF16)

    def ei_wait(d):
        for copy in ei_copies(d):
            copy.wait()

    act_copy.wait()
    ei_wait(2)
    t_dots(2, 1 - k, t_sib)
    t_dots(2, k, t_own)
    a_own_copy.wait()
    pl.semaphore_wait(barrier, expected)
    send(t_sib.at[2], t_sib_in.at[2], sib, t1 + 2)
    c1_send(0)
    spread_send()
    c2_send(0, 0)
    a_ring[0].start()
    for d in order[1:]:
        ei_wait(d)
        t_dots(d, 1 - k, t_sib)
        send(t_sib.at[d], t_sib_in.at[d], sib, t1 + d)
    t_join(2)
    t_sum.start()
    for d in order[1:]:
        t_dots(d, k, t_own)
    for d in order[1:]:
        t_join(d)
    arrived(c_spread, sp)
    c1_send(1)
    a1_send()
    c2_send(0, 1)
    arrived(c1_in.at[0], c1)
    c2_send(1, 0)
    s1_send()
    t_sum.pass_up()
    t_sum.pass_down()
    arrived(c1_in.at[1], c1 + 1)
    c2_send(1, 1)
    e1_send()

    def c_enter(j):
        if j == 0:
            arrived(c_all.at[k, y], c2)
        c_ring[j].start()
        send(c_block(k, j, y), c_block(k, j, y), sib, c4 + j)

    def c_pass(j):
        c_ring[j].pass_up()
        c_ring[j].pass_down()
        for d in (3, 1):
            send(c_block(k, j, ring(y, d)), c_block(k, j, ring(y, d)), sib, c4 + j)

    def c_finish(j):
        c_ring[j].finish()
        for half in (slice(0, 2), slice(2, 4)):
            send(c_block(k, j, ring(y, 2), half), c_block(k, j, ring(y, 2), half), sib, c4 + j)

    def c_sibling(j):
        arrived(c_all.at[1 - k, :, :, :, j * WIDE:(j + 1) * WIDE], c4 + j)

    def t_enter(c):
        rows = slice(c * 256, c * 256 + 256)
        arrived(t_swap_in.at[rows], t3 + c)
        t_all[y, rows] = (t_own[0, zh, rows] + t_swap_in[rows].astype(F32)).astype(BF16)
        t_ring[c].start()

    def g_block(j):
        parts = (
            (0, slice(None), a_all.at[0]),
            (1, slice(0, 64), a_all.at[1, :, 0:64]),
            (3, slice(64, 128), a_all.at[1, :, 64:128]),
        )
        for half in range(2):
            total = None
            for d, toks, acts in parts:
                block = jnp.concatenate(
                    [
                        c_block(kk, j, ring(2 * v + x1, d), toks=toks)[...].reshape(-1, WIDE)
                        for v in range(2)
                        for kk in range(2)
                    ],
                    axis=1,
                )
                part = dot(block, acts[:, :, half * 512:half * 512 + 512].reshape(-1, 512), ((0,), (0,)))
                total = part if total is None else total + part
            total = total.astype(BF16)
            for v in range(2):
                g_part[j, half * 2 + v] = total[v * 2 * WIDE:(v + 1) * 2 * WIDE]

    def g_enter(j):
        c_sibling(j)
        g_block(j)
        g_sum[j].start()

    def g_pass(j):
        g_sum[j].pass_up()
        g_sum[j].pass_down()

    def t_leave():
        t_sum.finish()
        for c in range(2):
            rows = slice(c * 256, c * 256 + 256)
            for half in range(2):
                t_own[0, half, rows] = (
                    t_part[y, half, rows].astype(F32)
                    + t_two[0, half, rows].astype(F32)
                    + t_two[1, half, rows].astype(F32)
                )
            t_swap[rows] = t_own[0, 1 - zh, rows].astype(BF16)
            send(t_swap.at[rows], t_swap_in.at[rows], z_far, t3 + c)

    def t_pass():
        for c in range(2):
            t_ring[c].pass_up()
            t_ring[c].pass_down()

    def both(gather):
        gather.pass_up()
        gather.pass_down()

    arrived(a_all.at[:, x, :, a_cols(1 - zh)], a1)
    a_ring[1].start()
    both(a_ring[0])
    c_enter(0)
    both(a_ring[1])
    t_leave()
    c_pass(0)
    c_enter(1)
    c_enter(2)
    arrived(s_all.at[:, x], s1)
    s_ring.start()
    c_finish(0)
    for ring_of_a in a_ring:
        ring_of_a.finish()
    g_enter(0)
    c_pass(1)
    t_enter(0)
    t_enter(1)
    c_pass(2)
    c_finish(1)
    g_pass(0)
    g_enter(1)
    t_pass()
    both(s_ring)
    e2_send()
    c_enter(3)
    c_finish(2)
    g_enter(2)
    g_pass(1)

    def u_dot(c, n):
        total = None
        for i in range(4):
            part = dot(
                t_all[i, c * 256:c * 256 + 256], s_all[n // 4, n % 4, :, i * 256:(i + 1) * 256], ((1,), (1,))
            )
            total = part if total is None else total + part
        return total

    for c in range(2):
        t_ring[c].finish()
        if c == 0:
            s_ring.finish()
        for n in range(8):
            u_own[c, n % 2, n // 2] = u_dot(c, n)
        u_sib[c] = u_own[c, 1 - k].astype(BF16)
        send(u_sib.at[c], u_sib_in.at[c], sib, u1 + c)
    e_enter(0)
    c_pass(3)
    for c in range(2):
        arrived(u_sib_in.at[c], u1 + c)
        u_part[c] = (u_own[c, k] + u_sib_in[c].astype(F32)).astype(BF16)
        for d in (2, 1, 3):
            send(u_part.at[c, ring(z, d)], u_in.at[c, d], at(z=ring(z, d)), u2 + c)
    g_pass(2)
    e_enter(1)
    c_finish(3)
    g_enter(3)

    def u_enter(c):
        rows = slice(c * 256, c * 256 + 256)
        arrived(u_in.at[c, 1:4], u2 + c)
        u_all[zl, rows, u_cols(k, y)] = (u_part[c, z].astype(F32) + u_in[c, 2].astype(F32)).astype(BF16)
        u_all[1 - zl, rows, u_cols(k, y)] = (u_in[c, 1].astype(F32) + u_in[c, 3].astype(F32)).astype(BF16)
        u_ring[c].start()
        send(u_block(c, k, y), u_block(c, k, y), sib, u4 + c)

    def u_pass(c):
        u_ring[c].pass_up()
        u_ring[c].pass_down()
        for d in (3, 1):
            send(u_block(c, k, ring(y, d)), u_block(c, k, ring(y, d)), sib, u4 + c)

    def u_finish(c):
        u_ring[c].finish()
        for n in range(2):
            half = u_block(c, k, ring(y, 2), n)
            send(half, half, sib, u4 + c)
        arrived(u_all.at[:, c * 256:c * 256 + 256, pl.ds(pl.multiple_of((1 - k) * 512, 512), 512)], u4 + c)

    u_enter(0)
    both(e_ring[0])
    u_enter(1)
    u_pass(0)
    both(e_ring[1])
    u_pass(1)
    g_pass(3)
    u_finish(0)
    for ring_of_e in e_ring:
        ring_of_e.finish()

    def o_shard(c, v, tok):
        for w in range(2):
            slot = 2 * y0 + v
            if w:
                slot = outer(slot)
            weight = e_all[slot].reshape(256, 1024)
            total = dot(u_all[tok, c * 256:c * 256 + 256], weight, ((1,), (1,))).astype(BF16)
            for n in range(2):
                o_part[c, v * 2 + tok, :, n * 256 + w * 128:n * 256 + w * 128 + 128] = total[:, n * 128:n * 128 + 128]

    def o_enter(c):
        o_shard(c, 1 - zh, zl)
        o_sum[c].start()
        for v, tok in ((zh, 1 - zl), (1 - zh, 1 - zl), (zh, zl)):
            o_shard(c, v, tok)

    o_enter(0)
    u_finish(1)
    o_enter(1)
    o_sum[0].pass_up()
    o_sum[0].pass_down()
    o_sum[1].pass_up()
    o_sum[1].pass_down()

    def last(dst, part, two, rows, first, to):
        @pl.loop(0, rows // 64)
        def _(i):
            src = pl.ds(pl.multiple_of(first + i * 64, 64), 64)
            dst[pl.ds(pl.multiple_of(to + i * 64, 64), 64)] = (
                part[src].astype(F32) + two[0, src].astype(F32) + two[1, src].astype(F32)
            ).astype(BF16)

    for j in range(PARTS):
        g_sum[j].finish()
        for kk in range(2):
            last(grad_ref, g_part.at[j, z], g_two.at[j], WIDE, kk * WIDE, kk * 512 + j * WIDE)
    for c in range(2):
        o_sum[c].finish()
        rows = slice(c * 256, c * 256 + 256)
        last(out_ref, o_part.at[c, z], o_two.at[c], 256, 0, c * 256)
    assert len(lone) <= LONE and len(loads) <= N_SEND - LONE
    for copy, when in lone:
        pl.when(when)(copy.wait_send)
    for n, size in enumerate(loads):
        rows = ei_hbm.at[0:size // 8192]
        remote(rows, rows, sib, LONE + n, 0).wait_send()


def per_device(small_weight, expand_out, expand_in, activations, cotangent):
    hbm = pl.BlockSpec(memory_space=pl.ANY)
    vmem = pl.BlockSpec(memory_space=pltpu.VMEM)

    def buf(*shape, dtype=BF16):
        return pltpu.VMEM(shape, dtype)

    return pl.pallas_call(
        kernel,
        out_shape=(
            pltpu.VMEM((512, 512), BF16),
            pltpu.VMEM((1024, 512), BF16),
        ),
        in_specs=[hbm] * 5,
        out_specs=(vmem, vmem),
        scratch_shapes=[
            buf(4, 4, 512, 256),
            buf(2, 2, 128, 512),
            pltpu.SemaphoreType.DMA((18,)),
            buf(2, 4, 128, 1024),
            buf(4, 64, 1024),
            buf(4, 4, 64, 1024),
            buf(2, 4, 128, 1024),
            buf(2, 4, 4, 128, 512),
            buf(2, 128, 512),
            buf(2, 128, 512),
            buf(4, 2, 512, 256),
            buf(4, 2, 512, 256),
            buf(4, 2, 512, 256, dtype=F32),
            buf(4, 2, 512, 256),
            buf(2, 512, 256),
            buf(2, 2, 512, 256),
            buf(512, 256),
            buf(512, 256),
            buf(4, 512, 256),
            buf(2, 2, 4, 256, 128, dtype=F32),
            buf(2, 4, 256, 128),
            buf(2, 4, 256, 128),
            buf(2, 4, 256, 128),
            buf(2, 4, 256, 128),
            buf(2, 512, 1024),
            buf(2, 4, 256, 512),
            buf(2, 2, 128, 512),
            buf(2, 2, 256, 512),
            buf(PARTS, 4, 2 * WIDE, 512),
            buf(PARTS, 2, WIDE, 512),
            buf(PARTS, 2, 2 * WIDE, 512),
            pltpu.SemaphoreType.DMA((N_SEND,)),
            pltpu.SemaphoreType.DMA((N_RECV,)),
        ],
        compiler_params=pltpu.CompilerParams(
            collective_id=0, has_side_effects=True, vmem_limit_bytes=58 * 2**20
        ),
        cost_estimate=pl.CostEstimate(flops=9_700_000_000, bytes_accessed=8_000_000, transcendentals=0),
        name="grow",
    )(
        small_weight,
        expand_out,
        expand_in,
        activations.reshape(2, 2, 128, 512),
        cotangent.reshape(2, 2, 128, 512),
    )

def solution(mesh):
    in_specs = (
        P(("row", "col"), None),
        P(("row", "col"), None),
        P("col", None),
        P("row", "col"),
        P("row", "col"),
    )
    out_specs = (P("row", "col"), P("row", "col"))
    return jax.shard_map(per_device, mesh=mesh, in_specs=in_specs, out_specs=out_specs, check_vma=False)
```
